256 devices in a mesh: particle: 16 (over x, y_lo, core), shard: 16 (over z, y_hi).
Axes of the slice: x: 4, y: 4 (y_hi: 2, y_lo: 2; y = y_hi * 2 + y_lo), z: 8, core: 2. Of those that a mesh axis runs over, the one named last changes fastest.
Arguments:
- pool: bfloat16 [16384, 1024], P('shard'), may hold values from -6 to 6
- batch_index: int32 [8192], P('shard'), may hold values from 0 to 1023
- kernel_scale: int32 [1], replicated, may hold values from 4194304 to 8388607
- cotangent: bfloat16 [16, 8192, 1024], P('particle', 'shard'), may hold values from -6 to 6
- weights: float32 [16, 1024, 2, 2048], P('particle', 'shard'), may hold values from -10 to 10
- first_moment: float32 [16, 1024, 2, 2048], P('particle', 'shard'), may hold values from -2 to 2
- second_moment: float32 [16, 1024, 2, 2048], P('particle', 'shard'), may hold values from 0.01 to 1
Outputs:
- new_weights: float32 [16, 1024, 2, 2048], P('particle', 'shard')
- new_first: float32 [16, 1024, 2, 2048], P('particle', 'shard')
- new_second: float32 [16, 1024, 2, 2048], P('particle', 'shard')
- transport: float32 [16, 1024, 2, 2048], P('particle', 'shard')
The draws below stay inside these ranges and needn't reach their ends.
Inputs may be any that keep to these rules, and one draw needn't show every extreme that they name: `batch_index`: each entry names a row of the pool block that the same index of shard holds.
All inputs are finite; a program needn't handle non-finite values.
Results may differ from the reference program's by a relative error of at most 0.015.
Values may be sent and summed in bfloat16 or wider, within the bound.
A program may use at most 192 MiB of HBM per device.

```python
import math
import jax
import jax.numpy as jnp
from jax import lax

D = 1024
FF = 2048
TOK_DEV = 512
POOL_DEV = 1024
PARTICLES = 16
TOKENS = 8192
POOL = 16384
PARAMS = 4194304


def draw_weights(key, part):
    base_key, noise_key, spread_key = jax.random.split(jax.random.fold_in(key, 17), 3)
    shape_full = (PARTICLES, D, 2, FF)
    shape_base = (1, D, 2, FF)
    row_pos = (jnp.arange(D, dtype=jnp.float32) + 0.5) / D - 0.5
    rise = jnp.exp(0.5 * jnp.log(3.0) * row_pos)[None, :, None, None]
    spread = jnp.exp(jax.random.uniform(spread_key, (PARTICLES, 1, 1, 1), jnp.float32, jnp.log(0.3), jnp.log(1.2)))
    base_part = jax.random.truncated_normal(base_key, -3.0, 3.0, shape_base, jnp.float32)
    noise_part = jax.random.truncated_normal(noise_key, -3.0, 3.0, shape_full, jnp.float32)
    return (base_part + spread * rise * noise_part).astype(jnp.float32)


def place_ends(entries, rng, low, largest):
    longest = entries.shape.index(max(entries.shape))
    spots = []
    for shift in (0, 1):
        where = [jax.random.randint(jax.random.fold_in(rng, axis), (), 0, length) for axis, length in enumerate(entries.shape)]
        where[longest] = (where[longest] + shift) % entries.shape[longest]
        spots.append(tuple(where))
    return entries.at[spots[0]].set(low).at[spots[1]].set(largest)


def levels(rng, dims, shards, least, top_value):
    factor_of = 1.0
    for axis_at, shards_of in shards:
        heights = jax.random.uniform(jax.random.fold_in(jax.random.fold_in(rng, 6), axis_at), (shards_of,), jnp.float32, least / len(shards), top_value / len(shards))
        factor_of = factor_of * jnp.repeat(jnp.exp(heights), dims[axis_at] // shards_of).reshape((-1,) + (1,) * (len(dims) - 1 - axis_at))
    return factor_of


def scatter_about(rng, shape, width, limit, cuts=(), held_as=jnp.bfloat16):
    array = jax.random.normal(rng, shape, jnp.float32) * width
    if len(cuts) > 0:
        array = levels(rng, shape, cuts, -0.22, 0.18) * array
    return jnp.clip(array, min=-limit, max=limit).astype(held_as)


def setup_inputs(seed: int = 0) -> dict:
    splits = jax.random.split(jax.random.key(seed), 8)
    pool = scatter_about(splits[0], (POOL, D), 1.0, 6.0, ((0, 16),))
    batch_index = place_ends(jax.random.randint(splits[1], (TOKENS,), 0, POOL_DEV), jax.random.fold_in(splits[1], 1), 0, POOL_DEV - 1).astype(jnp.int32)
    kernel_scale = jax.random.randint(splits[2], (1,), PARAMS, 2 * PARAMS).astype(jnp.int32)
    cotangent = scatter_about(splits[3], (PARTICLES, TOKENS, D), 1.0, 6.0, ((0, 16), (1, 16)))
    weights = draw_weights(jax.random.fold_in(splits[7], 71), 0)
    first_moment = scatter_about(splits[5], (PARTICLES, D, 2, FF), 0.3, 2.0, ((0, 16), (1, 16)), jnp.float32)
    second_moment = jnp.clip(jnp.exp(math.log(1.0) - 4.6051702 * jax.random.uniform(splits[6], (PARTICLES, D, 2, FF), jnp.float32) ** levels(splits[6], (PARTICLES, D, 2, FF), ((0, 16), (1, 16)), -0.2, 0.2)), 0.01, 1.0)
    return dict(pool=pool, batch_index=batch_index, kernel_scale=kernel_scale, cotangent=cotangent, weights=weights, first_moment=first_moment, second_moment=second_moment)


def gelu_pair(up_proj):
    cdf_part = 0.5 * (1.0 + jax.scipy.special.erf(up_proj * 0.7071067811865476))
    density = jnp.exp(-0.5 * up_proj * up_proj) * 0.3989422804014327
    return (up_proj * cdf_part, cdf_part + up_proj * density)

def reference(pool, batch_index, kernel_scale, cotangent, weights, first_moment, second_moment):
    offsets = jnp.arange(TOKENS, dtype=jnp.int32) // TOK_DEV * POOL_DEV
    picked = pool[(batch_index + offsets).astype(jnp.int32)].astype(jnp.float32)
    normed = (picked * lax.rsqrt(lax.optimization_barrier(jnp.mean(picked * picked, axis=1, keepdims=True)) + 1e-06)).astype(jnp.bfloat16)
    grad_scale = 1.0 / (TOKENS * D)

    def particle_score(particle_pair):
        particle_w, upstream = particle_pair
        wb_rows = particle_w.astype(jnp.bfloat16)
        up_proj = jnp.dot(normed, wb_rows[:, 0, :], preferred_element_type=jnp.float32) * D ** (-0.5)
        back_proj = jnp.dot(upstream, wb_rows[:, 1, :], preferred_element_type=jnp.float32) * FF ** (-0.5)
        act_full, gelu_slope = gelu_pair(up_proj)
        activation = act_full.astype(jnp.bfloat16)
        up_grad = (back_proj * gelu_slope).astype(jnp.bfloat16)
        g_up = jnp.dot(normed.T, up_grad, preferred_element_type=jnp.float32) * (D ** (-0.5) * grad_scale)
        g_down = jnp.dot(upstream.T, activation, preferred_element_type=jnp.float32) * (FF ** (-0.5) * grad_scale)
        return (-jnp.stack([g_up, g_down], axis=1)).astype(jnp.bfloat16)
    scores = lax.map(particle_score, (weights, cotangent))
    inverse_band = 1.0 / kernel_scale[0].astype(jnp.float32)
    repulse = 2.0 * inverse_band
    rounded_w = lax.optimization_barrier(weights.astype(jnp.bfloat16)).astype(jnp.float32)

    def distance_row(own_row):
        offset_sq = own_row[None] - rounded_w
        return lax.optimization_barrier(jnp.sum(offset_sq * offset_sq, axis=(1, 2, 3)))
    distances = lax.map(distance_row, rounded_w)
    kernel = jnp.exp(-distances * inverse_band)
    pushed_field = scores.astype(jnp.float32) - repulse * rounded_w

    def weighted_row(kernel_row):
        term_rows = (kernel_row[:, None, None, None] * pushed_field).astype(jnp.bfloat16)
        return lax.optimization_barrier(jnp.sum(lax.optimization_barrier(term_rows).astype(jnp.float32), axis=0))
    weighted = lax.map(weighted_row, kernel)
    kernel_total = lax.optimization_barrier(jnp.sum(kernel, axis=1))[:, None, None, None]
    transport = PARAMS / PARTICLES * (weighted + repulse * kernel_total * rounded_w)
    new_first = 0.9 * first_moment - 0.1 * transport
    new_second = 0.999 * second_moment + 0.001 * transport * transport
    new_weights = weights - 0.01 * new_first / (jnp.sqrt(new_second) + 1e-08)
    return (new_weights, new_first, new_second, transport)
```

```python
import functools

import jax
import jax.numpy as jnp
from jax import lax
from jax.experimental import pallas as pl
from jax.experimental.pallas import tpu as pltpu
from jax.sharding import PartitionSpec as P

MESH = pl.DeviceIdType.MESH
CHUNKS = 2
LANES = 128
HIGHEST = lax.Precision.HIGHEST
F32 = jnp.float32
BF16 = jnp.bfloat16


def gelu_pair(up_proj):
    cdf_part = 0.5 * (1.0 + lax.erf(up_proj * 0.7071067811865476))
    density = jnp.exp(-0.5 * up_proj * up_proj) * 0.3989422804014327
    return (up_proj * cdf_part, cdf_part + up_proj * density)


def remote(src, dst, send_sem, recv_sem, device):
    return pltpu.make_async_remote_copy(
        src_ref=src,
        dst_ref=dst,
        send_sem=send_sem,
        recv_sem=recv_sem,
        device_id=device,
        device_id_type=MESH,
    )


def stein_kernel(
    dims,
    scale_ref, idx_ref, w_hbm, pool_hbm, cot_hbm,
    out_ref,
    wf, poolv, wbr, wba, wg, na, ca, nt, ct, act, upg, rss, rsr, sc, sa, wa, fld, tr, ta,
    d1, dmine, dpart, dpair, dring, krep,
    load_sem, ex_s, ex_r, cot_s, cot_r, cot_fs, cot_fr, nseg_s, nseg_r, nb_s, nb_r,
    wa_s, wa_r, ag_s, ag_r, rs_s, rs_r, dp_s, dp_r, dh_s, dh_r, dz_s, dz_r, sa_s, sa_r, ta_s, ta_r,
):
    NP, NZ, RB, TOK, D, FF, POOL = dims
    NXY, NX = NP // 2, NP // 4
    G = NX * 2
    NT = FF // LANES
    TC = NT // 2 // CHUNKS
    CH = TC * LANES
    SEG = TOK // G
    HT = TOK // 2
    rem = lax.rem
    p, s = lax.axis_index("particle"), lax.axis_index("shard")
    c, xy = rem(p, 2), p // 2
    x, yl = xy // 2, rem(xy, 2)
    h, z = rem(s, 2), s // 2
    zdev = (
        (p, rem(z + 1, NZ) * 2 + h),
        (p, rem(z + NZ - 1, NZ) * 2 + h),
    )
    sibling = (xy * 2 + 1 - c, s)
    across = (p, z * 2 + 1 - h)
    diagonal = (xy * 2 + 1 - c, z * 2 + 1 - h)
    role = xy * 2 + h

    load_w = pltpu.make_async_copy(w_hbm, wf, load_sem.at[0])
    load_w.start()
    load_pool = pltpu.make_async_copy(pool_hbm, poolv, load_sem.at[1])
    load_pool.start()
    barrier = pltpu.get_barrier_semaphore()

    def greet(device):
        pl.semaphore_signal(barrier, inc=1, device_id=device, device_id_type=MESH)

    greet(zdev[0])
    greet(zdev[1])
    greet(diagonal)

    @pl.loop(1, NP)
    def _(d):
        greet((rem(p + d, NP), s))

    @pl.loop(0, NXY)
    def _(o):
        greet((o * 2 + c, z * 2 + 1 - h))

    load_w.wait()
    for half in range(2):
        for k in range(CHUNKS):
            for tile in range(TC):
                for j in range(2):
                    t = (half * CHUNKS + k) * TC + tile
                    v = wf[pl.ds(2 * t + j, RB, stride=2 * NT), :].astype(BF16)
                    wbr[half, k, j, :, tile * LANES:(tile + 1) * LANES] = v
                    wba[(tile * 2 + j) * 2 + half, k * RB:(k + 1) * RB, :] = v
    pl.semaphore_wait(barrier, NP + NXY + 2)

    own_rows = pl.ds(pl.multiple_of((z * 2 + h) * RB, RB), RB)
    sub_at_dest = rem(h + c, 2)

    def exchange(k, half, device):
        return remote(
            wbr.at[half, k], wg.at[k, :, own_rows, :],
            ex_s.at[k * 2 + half], ex_r.at[k * 2 + sub_at_dest], device,
        )

    def cot_half(half):
        part = cot_hbm.at[pl.ds(half * HT, HT)]
        return remote(part, ca.at[h, pl.ds(half * HT, HT)], cot_s.at[half], cot_r.at[1],
                      (xy * 2 + half, z * 2 + 1 - h))

    cot_load = pltpu.make_async_copy(cot_hbm, ca.at[h], load_sem.at[2])
    cot_full = remote(cot_hbm, ca.at[h], cot_s.at[0], cot_r.at[0], sibling)

    @pl.when(c == h)
    def _():
        for k in range(CHUNKS):
            exchange(k, 1 - c, sibling).start()
        for k in range(CHUNKS):
            wg[k, :, own_rows, :] = wbr[c, k]
        cot_load.start()
        cot_full.start()

    @pl.when(c != h)
    def _():
        for k in range(CHUNKS):
            for half in range(2):
                exchange(k, half, (xy * 2 + half, z * 2 + 1 - h)).start()
        for half in range(2):
            cot_half(half).start()

    def exchange_wait(k, sub):
        rows = pl.ds(pl.multiple_of((z * 2 + rem(h + sub, 2)) * RB, RB), RB)
        remote(wbr.at[0, k], wg.at[k, :, rows, :], ex_s.at[0], ex_r.at[k * 2 + sub], sibling).wait_recv()

    def ag(k, j, step, sub):
        b = rem(z + NZ - step, NZ) if j == 0 else rem(z + step, NZ)
        rows = pl.ds(pl.multiple_of((b * 2 + rem(h + sub, 2)) * RB, RB), RB)
        n = ((k * 2 + j) * (NZ - 1) + step) * 2 + sub
        return remote(wg.at[k, j, rows, :], wg.at[k, j, rows, :], ag_s.at[n], ag_r.at[n], zdev[j])

    def ag_wait(k, j, step, sub):
        b = rem(z + 2 * NZ - 1 - step, NZ) if j == 0 else rem(z + 1 + step, NZ)
        rows = pl.ds(pl.multiple_of((b * 2 + rem(h + sub, 2)) * RB, RB), RB)
        n = ((k * 2 + j) * (NZ - 1) + step) * 2 + sub
        remote(wg.at[k, j, rows, :], wg.at[k, j, rows, :], ag_s.at[n], ag_r.at[n], zdev[j]).wait_recv()

    def ag_relay(k, step, last=None):
        for sub in range(2):
            for j in range(2):
                ag_wait(k, j, step, sub)
                if last is None:
                    @pl.when(step < NZ - 2)
                    def _():
                        ag(k, j, step + 1, sub).start()
                elif not last:
                    ag(k, j, step + 1, sub).start()

    for k in range(CHUNKS):
        @pl.when(c != h)
        def _():
            exchange_wait(k, 0)
        for j in range(2):
            ag(k, j, 0, 0).start()

    load_pool.wait()
    TB = min(LANES, TOK)

    @pl.loop(0, TOK // TB)
    def _(blk):
        at = pl.multiple_of(blk * TB, TB)
        col = jnp.broadcast_to(idx_ref[:, pl.ds(at, TB)], (LANES, TB)).T
        lane = lax.broadcasted_iota(jnp.int32, (TB, LANES), 1)
        onehot = jnp.concatenate(
            [jnp.where(col == lane + i * LANES, 1.0, 0.0).astype(BF16) for i in range(POOL // LANES)], axis=1
        )
        picked = jnp.dot(onehot, poolv[...], preferred_element_type=F32)
        mean = jnp.mean(picked * picked, axis=1, keepdims=True)
        na[h, pl.ds(at, TB), :] = (picked * lax.rsqrt(mean + 1e-06)).astype(BF16)

    seg = x * 2 + c
    own_seg = na.at[h, pl.ds(pl.multiple_of(seg * SEG, SEG), SEG)]
    nseg = remote(own_seg, own_seg, nseg_s, nseg_r, across)
    nseg.start()

    for k in range(CHUNKS):
        exchange_wait(k, 1)
        for j in range(2):
            ag(k, j, 0, 1).start()

    def slice_out(d):
        q = rem(p + d, NP)
        return remote(wba.at[q], wa.at[p], wa_s.at[d], wa_r.at[d], (q, s))

    def slice_wait(d):
        q = rem(p + NP - d, NP)
        remote(wba.at[q], wa.at[q], wa_s.at[d], wa_r.at[d], (q, s)).wait_recv()

    @pl.loop(1, NP)
    def _(d):
        slice_out(d).start()

    wa[p] = wba[p]

    got_seg = na.at[1 - h, pl.ds(pl.multiple_of(seg * SEG, SEG), SEG)]

    def seg_out(d):
        g = rem(seg + d, G)
        return remote(got_seg, got_seg, nb_s.at[d], nb_r.at[d], ((g // 2 * 2 + yl) * 2 + rem(g, 2), s))

    def seg_wait(d):
        g = rem(seg + G - d, G)
        part = na.at[1 - h, pl.ds(pl.multiple_of(g * SEG, SEG), SEG)]
        remote(part, part, nb_s.at[d], nb_r.at[d], sibling).wait_recv()

    def share_segments():
        remote(got_seg, got_seg, nseg_s, nseg_r, across).wait_recv()

        @pl.loop(1, G)
        def _(d):
            seg_out(d).start()

    cot_mine = ca.at[1 - h, pl.ds(pl.multiple_of(c * HT, HT), HT)]
    cot_other = ca.at[1 - h, pl.ds(pl.multiple_of((1 - c) * HT, HT), HT)]
    cot_pass = remote(cot_mine, cot_mine, cot_fs, cot_fr, sibling)

    def pass_cotangent():
        remote(cot_mine, cot_mine, cot_s.at[0], cot_r.at[1], sibling).wait_recv()
        cot_pass.start()

    eye = lax.broadcasted_iota(jnp.int32, (NP, LANES), 0) == lax.broadcasted_iota(jnp.int32, (NP, LANES), 1)

    def part_out(d):
        q = rem(p + d, NP)
        return remote(dmine, dpart.at[p], dp_s.at[d], dp_r.at[d], (q, s))

    def part_wait(d):
        q = rem(p + NP - d, NP)
        remote(dmine, dpart.at[q], dp_s.at[d], dp_r.at[d], (q, s)).wait_recv()

    def partial_distances():
        @pl.loop(1, NP)
        def _(d):
            slice_wait(d)

        @pl.loop(0, NP)
        def _(i):
            own = wa[i].astype(F32)
            for j in range(NP):
                off = own - wa[j].astype(F32)
                d1[i, j:j + 1, :] = jnp.sum(off * off, axis=0, keepdims=True)

        flat = d1[...].reshape(NP * NP, LANES)
        spread = jnp.dot(flat, jnp.ones((LANES, LANES), F32), precision=HIGHEST, preferred_element_type=F32)
        for i in range(NP):
            dmine[i:i + 1, :] = jnp.sum(
                jnp.where(eye, spread[i * NP:(i + 1) * NP, :], 0.0), axis=0, keepdims=True
            )

        @pl.loop(1, NP)
        def _(d):
            part_out(d).start()

    pair_out = remote(dpair.at[0], dpair.at[1], dh_s, dh_r, across)

    def pair_distances():
        dpart[p] = dmine[...]

        @pl.loop(1, NP)
        def _(d):
            part_wait(d)

        dpair[0] = jnp.sum(dpart[...], axis=0)
        pair_out.start()

    def ring_out(step):
        b = rem(z + NZ - step, NZ)
        return remote(dring.at[b], dring.at[b], dz_s.at[step], dz_r.at[step], zdev[0])

    def ring_wait(step):
        b = rem(z + 2 * NZ - 1 - step, NZ)
        remote(dring.at[b], dring.at[b], dz_s.at[step], dz_r.at[step], zdev[0]).wait_recv()

    def ring_start():
        pair_out.wait_recv()
        dring[z] = dpair[0] + dpair[1]
        ring_out(0).start()

    def ring_relay(step, last=None):
        ring_wait(step)
        if last is None:
            @pl.when(step < NZ - 2)
            def _():
                ring_out(step + 1).start()
        elif not last:
            ring_out(step + 1).start()

    inverse_band = 1.0 / jnp.full((1, LANES), scale_ref[0], jnp.int32).astype(F32)
    repulse = 2.0 * inverse_band

    def kernel_matrix():
        near = jnp.exp(-jnp.sum(dring[...], axis=0) * inverse_band)
        for i in range(NP):
            d1[i] = jnp.where(eye, jnp.broadcast_to(near[i:i + 1, :], (NP, LANES)), 0.0)
        flat = d1[...].reshape(NP * NP, LANES)
        spread = jnp.dot(flat, jnp.ones((LANES, LANES), F32), precision=HIGHEST, preferred_element_type=F32)
        krep[...] = spread.reshape(NP, NP, LANES)

    def hidden(k, blk, flip):
        hb = rem(h + blk // 2, 2)
        at = pl.multiple_of(rem(blk, 2) * HT, HT)
        normed = na[hb, pl.ds(at, HT), :]
        upstream = ca[hb, pl.ds(at, HT), :]
        rows = pl.multiple_of(hb * TOK + at, HT)
        up_proj = jnp.dot(normed, wg[k, 0], preferred_element_type=F32) * D ** (-0.5)
        back_proj = jnp.dot(upstream, wg[k, 1], preferred_element_type=F32) * FF ** (-0.5)
        act_full, gelu_slope = gelu_pair(up_proj)
        act[k, pl.ds(rows, HT), :] = act_full.astype(BF16)
        upg[k, pl.ds(rows, HT), :] = (back_proj * gelu_slope).astype(BF16)
        if flip:
            nt[:, pl.ds(rows, HT)] = normed.T
            ct[:, pl.ds(rows, HT)] = upstream.T

    def gradient(k, j, b):
        lhs = (nt if j == 0 else ct)[pl.ds(pl.multiple_of(b * 2 * RB, 2 * RB), 2 * RB), :]
        return jnp.dot(lhs, (upg if j == 0 else act)[k], preferred_element_type=F32)

    def rs(k, j, step, sub):
        n = ((k * 2 + j) * (NZ - 1) + step) * 2 + sub
        return remote(rss.at[n], rsr.at[n], rs_s.at[n], rs_r.at[n], zdev[j])

    def rs_step(k, step, first=False):
        parts = [
            gradient(k, 0, rem(z + 2 * NZ - 1 - step, NZ)),
            gradient(k, 1, rem(z + 1 + step, NZ)),
        ]
        for sub in range(2):
            for j in range(2):
                total = parts[j][sub * RB:(sub + 1) * RB, :]
                n = ((k * 2 + j) * (NZ - 1) + step) * 2 + sub
                if not first:
                    rs(k, j, step - 1, sub).wait_recv()
                    total = total + rsr[n - 2].astype(F32)
                rss[n] = total.astype(BF16)
                rs(k, j, step, sub).start()

    grad_scale = 1.0 / (TOK * NZ * 2 * D)

    def rs_final(k):
        for j in range(2):
            part = gradient(k, j, z)
            factor = (D if j == 0 else FF) ** (-0.5) * grad_scale
            for sub in range(2):
                n = ((k * 2 + j) * (NZ - 1) + NZ - 2) * 2 + sub
                rs(k, j, NZ - 2, sub).wait_recv()
                total = part[sub * RB:(sub + 1) * RB, :] + rsr[n].astype(F32)
                score = (total * -factor).astype(BF16)
                for tile in range(TC):
                    sc[k, sub, tile * 2 + j] = score[:, tile * LANES:(tile + 1) * LANES]

    def score_out(k, d):
        r = rem(role + d, NP)
        return remote(sc.at[k, rem(r, 2), r // 2], sa.at[k, role], sa_s.at[k * NP + d], sa_r.at[k * NP + d],
                      (r // 2 * 2 + c, z * 2 + rem(r, 2)))

    def score_wait(k, d):
        r = rem(role + NP - d, NP)
        remote(sc.at[k, 0, 0], sa.at[k, r], sa_s.at[k * NP + d], sa_r.at[k * NP + d], sibling).wait_recv()

    def send_scores(k):
        @pl.loop(1, NP)
        def _(d):
            score_out(k, d).start()

        sa[k, role] = sc[k, h, xy]

    def transport_out(k, d):
        q = rem(p + d, NP)
        return remote(tr.at[k, q], ta.at[k, p], ta_s.at[k * NP + d], ta_r.at[k * NP + d], (q, s))

    def transport_wait(k, d):
        q = rem(p + NP - d, NP)
        remote(tr.at[k, 0], ta.at[k, q], ta_s.at[k * NP + d], ta_r.at[k * NP + d], sibling).wait_recv()

    params_total = 2 * D * FF

    def move(k):
        @pl.loop(1, NP)
        def _(d):
            score_wait(k, d)

        for q in range(NP):
            fld[q] = sa[k, q].astype(F32) - repulse * wa[q, k * RB:(k + 1) * RB, :].astype(F32)

        @pl.loop(0, NP)
        def _(i):
            weighted = krep[i, 0:1, :] * fld[0]
            for j in range(1, NP):
                weighted = weighted + krep[i, j:j + 1, :] * fld[j]
            kernel_total = jnp.sum(krep[i], axis=0, keepdims=True)
            own_w = wa[i, k * RB:(k + 1) * RB, :].astype(F32)
            tr[k, i] = (params_total / NP * (weighted + repulse * kernel_total * own_w)).astype(BF16)

        @pl.loop(1, NP)
        def _(d):
            transport_out(k, d).start()

        ta[k, p] = tr[k, p]

    def collect(k):
        @pl.loop(1, NP)
        def _(d):
            transport_wait(k, d)

        for q in range(NP):
            o, half = q // 2, q % 2
            t = (half * CHUNKS + k) * TC + o // 2
            out_ref[pl.ds(2 * t + o % 2, RB, stride=2 * NT), :] = ta[k, q].astype(F32)

    LAST = NZ - 2
    for step in range(NZ - 1):
        ag_relay(0, step, step == LAST)
        if step == min(3, LAST):
            share_segments()
        if step == min(4, LAST):
            partial_distances()
    pair_distances()
    pass_cotangent()

    @pl.when(c == h)
    def _():
        cot_load.wait()

    @pl.when(c != h)
    def _():
        remote(cot_hbm, ca.at[h], cot_s.at[0], cot_r.at[0], sibling).wait_recv()

    ring_start()
    EARLY = min(4, NZ - 1)

    @pl.loop(0, 4)
    def _(blk):
        @pl.when(blk == 2)
        def _():
            @pl.loop(1, G)
            def _(d):
                seg_wait(d)

            remote(cot_other, cot_other, cot_fs, cot_fr, sibling).wait_recv()

        hidden(0, blk, True)

        @pl.when(blk < EARLY)
        def _():
            ag_relay(1, blk)
            ring_relay(blk)

    rs_step(0, 0, True)
    for step in range(EARLY, NZ - 1):
        ag_relay(1, step, step == LAST)
        ring_relay(step, step == LAST)
        rs_step(0, step - EARLY + 1)
    kernel_matrix()
    DONE = NZ - 1 - EARLY

    @pl.loop(0, 4)
    def _(blk):
        hidden(1, blk, False)

        @pl.when(DONE + 1 + blk <= LAST)
        def _():
            rs_step(0, DONE + 1 + blk)

    rs_step(1, 0, True)
    rs_final(0)
    send_scores(0)
    for step in range(1, NZ - 1):
        rs_step(1, step)
        if step == min(3, LAST):
            move(0)
        if step == min(6, LAST):
            collect(0)
    rs_final(1)
    send_scores(1)
    move(1)
    collect(1)

    @pl.when(c == h)
    def _():
        for k in range(CHUNKS):
            exchange(k, 1 - c, sibling).wait_send()
        cot_full.wait_send()

    @pl.when(c != h)
    def _():
        for k in range(CHUNKS):
            for half in range(2):
                exchange(k, half, (xy * 2 + half, z * 2 + 1 - h)).wait_send()
        for half in range(2):
            cot_half(half).wait_send()

    nseg.wait_send()
    cot_pass.wait_send()
    pair_out.wait_send()

    @pl.loop(1, G)
    def _(d):
        seg_out(d).wait_send()

    @pl.loop(1, NP)
    def _(d):
        slice_out(d).wait_send()
        part_out(d).wait_send()
        for k in range(CHUNKS):
            score_out(k, d).wait_send()
            transport_out(k, d).wait_send()

    @pl.loop(0, NZ - 1)
    def _(step):
        ring_out(step).wait_send()
        for k in range(CHUNKS):
            for j in range(2):
                for sub in range(2):
                    ag(k, j, step, sub).wait_send()
                    rs(k, j, step, sub).wait_send()


def stein_transport(NP, NS, kernel_scale, batch_index, flat_w, pool, cotangent):
    NZ = NS // 2
    TOK, D = cotangent.shape
    RB = D // NS
    FF = flat_w.shape[0] * LANES // RB // 2
    POOL = pool.shape[0]
    NXY, G = NP // 2, NP // 2
    TC = FF // LANES // 2 // CHUNKS
    CH = TC * LANES
    assert TC * 2 == NXY
    dma = pltpu.SemaphoreType.DMA
    ring = CHUNKS * 2 * (NZ - 1) * 2
    scratch = [
        pltpu.VMEM(flat_w.shape, F32),
        pltpu.VMEM((POOL, D), BF16),
        pltpu.VMEM((2, CHUNKS, 2, RB, CH), BF16),
        pltpu.VMEM((NP, CHUNKS * RB, LANES), BF16),
        pltpu.VMEM((CHUNKS, 2, D, CH), BF16),
        pltpu.VMEM((2, TOK, D), BF16),
        pltpu.VMEM((2, TOK, D), BF16),
        pltpu.VMEM((D, 2 * TOK), BF16),
        pltpu.VMEM((D, 2 * TOK), BF16),
        pltpu.VMEM((CHUNKS, 2 * TOK, CH), BF16),
        pltpu.VMEM((CHUNKS, 2 * TOK, CH), BF16),
        pltpu.VMEM((ring, RB, CH), BF16),
        pltpu.VMEM((ring, RB, CH), BF16),
        pltpu.VMEM((CHUNKS, 2, NXY, RB, LANES), BF16),
        pltpu.VMEM((CHUNKS, NP, RB, LANES), BF16),
        pltpu.VMEM((NP, CHUNKS * RB, LANES), BF16),
        pltpu.VMEM((NP, RB, LANES), F32),
        pltpu.VMEM((CHUNKS, NP, RB, LANES), BF16),
        pltpu.VMEM((CHUNKS, NP, RB, LANES), BF16),
        pltpu.VMEM((NP, NP, LANES), F32),
        pltpu.VMEM((NP, LANES), F32),
        pltpu.VMEM((NP, NP, LANES), F32),
        pltpu.VMEM((2, NP, LANES), F32),
        pltpu.VMEM((NZ, NP, LANES), F32),
        pltpu.VMEM((NP, NP, LANES), F32),
        dma((3,)),
        dma((2 * CHUNKS,)), dma((2 * CHUNKS,)),
        dma((2,)), dma((2,)), dma(()), dma(()),
        dma(()), dma(()), dma((G,)), dma((G,)),
        dma((NP,)), dma((NP,)),
        dma((ring,)), dma((ring,)), dma((ring,)), dma((ring,)),
        dma((NP,)), dma((NP,)), dma(()), dma(()),
        dma((NZ - 1,)), dma((NZ - 1,)),
        dma((CHUNKS * NP,)), dma((CHUNKS * NP,)), dma((CHUNKS * NP,)), dma((CHUNKS * NP,)),
    ]
    anywhere = pl.BlockSpec(memory_space=pl.ANY)
    vmem = pl.BlockSpec(memory_space=pltpu.VMEM)
    return pl.pallas_call(
        functools.partial(stein_kernel, (NP, NZ, RB, TOK, D, FF, POOL)),
        out_shape=jax.ShapeDtypeStruct(flat_w.shape, F32),
        in_specs=[pl.BlockSpec(memory_space=pltpu.SMEM), vmem, anywhere, anywhere, anywhere],
        out_specs=vmem,
        scratch_shapes=scratch,
        compiler_params=pltpu.CompilerParams(
            collective_id=0, has_side_effects=True, vmem_limit_bytes=60 * 1024 * 1024
        ),
        name="stein",
    )(kernel_scale, batch_index.reshape(1, TOK), flat_w, pool, cotangent)


def local(NP, NS, pool, batch_index, kernel_scale, cotangent, weights, first_moment, second_moment):
    rows, pair, hidden_units = weights.shape[1:]

    def flatten(a):
        return a.reshape(rows, pair, hidden_units // LANES, LANES).transpose(0, 2, 1, 3).reshape(-1, LANES)

    def unflatten(a):
        a = a.reshape(rows, hidden_units // LANES, pair, LANES).transpose(0, 2, 1, 3)
        return a.reshape(1, rows, pair, hidden_units)

    flat_w = flatten(weights[0])
    transport = stein_transport(NP, NS, kernel_scale, batch_index, flat_w, pool, cotangent[0])
    new_first = 0.9 * flatten(first_moment[0]) - 0.1 * transport
    new_second = 0.999 * flatten(second_moment[0]) + 0.001 * transport * transport
    new_weights = flat_w - 0.01 * new_first / (jnp.sqrt(new_second) + 1e-08)
    return tuple(unflatten(a) for a in (new_weights, new_first, new_second, transport))


def solution(mesh):
    placed = (
        P("shard", None),
        P("shard"),
        P(),
        P("particle", "shard", None),
        P("particle", "shard", None, None),
        P("particle", "shard", None, None),
        P("particle", "shard", None, None),
    )
    return jax.shard_map(
        functools.partial(local, mesh.shape["particle"], mesh.shape["shard"]),
        mesh=mesh,
        in_specs=placed,
        out_specs=(P("particle", "shard", None, None),) * 4,
        check_vma=False,
    )
```

```python
import functools

import jax
import jax.numpy as jnp
from jax import lax
from jax.experimental import pallas as pl
from jax.experimental.pallas import tpu as pltpu
from jax.sharding import PartitionSpec as P

MESH = pl.DeviceIdType.MESH
CHUNKS = 2
LANES = 128
HIGHEST = lax.Precision.HIGHEST
F32 = jnp.float32
BF16 = jnp.bfloat16


def gelu_pair(up_proj):
    cdf_part = 0.5 * (1.0 + lax.erf(up_proj * 0.7071067811865476))
    density = jnp.exp(-0.5 * up_proj * up_proj) * 0.3989422804014327
    return (up_proj * cdf_part, cdf_part + up_proj * density)


def remote(src, dst, send_sem, recv_sem, device):
    return pltpu.make_async_remote_copy(
        src_ref=src,
        dst_ref=dst,
        send_sem=send_sem,
        recv_sem=recv_sem,
        device_id=device,
        device_id_type=MESH,
    )


def stein_kernel(
    dims,
    scale_ref, idx_ref, w_hbm, pool_hbm, cot_hbm,
    out_ref,
    wf, poolv, wbr, wba, wg, na, ca, nt, ct, act, upg, rss, rsr, sc, sa, wa, fld, tr, ta,
    d1, dmine, dpart, dpair, krep,
    load_sem, ex_s, ex_r, cot_s, cot_r, cot_fs, cot_fr, nseg_s, nseg_r, nb_s, nb_r,
    wa_s, wa_r, ag_s, ag_r, rs_s, rs_r, dp_s, dp_r, dh_s, dh_r, sa_s, sa_r, ta_s, ta_r,
):
    NP, NS, RB, TOK, D, FF, POOL = dims
    NZ = NS // 2
    NXY, NX = NP // 2, NP // 4
    G = NX * 2
    NT = FF // LANES
    TC = NT // 2 // CHUNKS
    CH = TC * LANES
    SEG = TOK // G
    HT = TOK // 2
    rem = lax.rem
    p, s = lax.axis_index("particle"), lax.axis_index("shard")
    c, xy = rem(p, 2), p // 2
    x, yl = xy // 2, rem(xy, 2)
    h, z = rem(s, 2), s // 2
    zdev = (
        (p, rem(z + 1, NZ) * 2 + h),
        (p, rem(z + NZ - 1, NZ) * 2 + h),
    )
    sibling = (xy * 2 + 1 - c, s)
    across = (p, z * 2 + 1 - h)
    diagonal = (xy * 2 + 1 - c, z * 2 + 1 - h)
    role = xy * 2 + h

    load_w = pltpu.make_async_copy(w_hbm, wf, load_sem.at[0])
    load_w.start()
    load_pool = pltpu.make_async_copy(pool_hbm, poolv, load_sem.at[1])
    load_pool.start()
    barrier = pltpu.get_barrier_semaphore()

    def greet(device):
        pl.semaphore_signal(barrier, inc=1, device_id=device, device_id_type=MESH)

    greet(zdev[0])
    greet(zdev[1])
    greet(diagonal)
    for bit in range(1, NZ.bit_length() - 1):
        greet((p, s + (2 << bit) - (4 << bit) * rem(z // (1 << bit), 2)))

    @pl.loop(1, NP)
    def _(d):
        greet((rem(p + d, NP), s))

    @pl.loop(0, NXY)
    def _(o):
        greet((o * 2 + c, z * 2 + 1 - h))

    load_w.wait()
    for half in range(2):
        for k in range(CHUNKS):
            for tile in range(TC):
                for j in range(2):
                    t = (half * CHUNKS + k) * TC + tile
                    v = wf[pl.ds(2 * t + j, RB, stride=2 * NT), :].astype(BF16)
                    wbr[half, k, j, :, tile * LANES:(tile + 1) * LANES] = v
                    wba[(tile * 2 + j) * 2 + half, k * RB:(k + 1) * RB, :] = v
    pl.semaphore_wait(barrier, NP + NXY + NZ.bit_length())

    own_rows = pl.ds(pl.multiple_of((z * 2 + h) * RB, RB), RB)
    sub_at_dest = rem(h + c, 2)

    def exchange(k, half, device):
        return remote(
            wbr.at[half, k], wg.at[k, :, own_rows, :],
            ex_s.at[k * 2 + half], ex_r.at[k * 2 + sub_at_dest], device,
        )

    def cot_half(half):
        part = cot_hbm.at[pl.ds(half * HT, HT)]
        return remote(part, ca.at[h, pl.ds(half * HT, HT)], cot_s.at[half], cot_r.at[1],
                      (xy * 2 + half, z * 2 + 1 - h))

    cot_load = pltpu.make_async_copy(cot_hbm, ca.at[h], load_sem.at[2])
    cot_full = remote(cot_hbm, ca.at[h], cot_s.at[0], cot_r.at[0], sibling)

    @pl.when(c == h)
    def _():
        for k in range(CHUNKS):
            exchange(k, 1 - c, sibling).start()
        for k in range(CHUNKS):
            wg[k, :, own_rows, :] = wbr[c, k]
        cot_load.start()
        cot_full.start()

    @pl.when(c != h)
    def _():
        for k in range(CHUNKS):
            for half in range(2):
                exchange(k, half, (xy * 2 + half, z * 2 + 1 - h)).start()
        for half in range(2):
            cot_half(half).start()

    def exchange_wait(k, sub):
        rows = pl.ds(pl.multiple_of((z * 2 + rem(h + sub, 2)) * RB, RB), RB)
        remote(wbr.at[0, k], wg.at[k, :, rows, :], ex_s.at[0], ex_r.at[k * 2 + sub], sibling).wait_recv()

    FAR = NZ // 2

    def hops(j, way):
        return FAR if j == way else NZ - 1 - FAR

    def slot(k, j, way, step, sub):
        return (((k * 2 + j) * 2 + way) * FAR + step) * 2 + sub

    def ag_copy(k, j, way, step, sub, back):
        b = rem(z + 2 * NZ - step - back, NZ) if way == 0 else rem(z + step + back, NZ)
        rows = pl.ds(pl.multiple_of((b * 2 + rem(h + sub, 2)) * RB, RB), RB)
        n = slot(k, j, way, step, sub)
        return remote(wg.at[k, j, rows, :], wg.at[k, j, rows, :], ag_s.at[n], ag_r.at[n], zdev[way])

    def ag(k, j, way, step, sub):
        return ag_copy(k, j, way, step, sub, 0)

    def ag_first(k, sub):
        for way in range(2):
            for j in range(2):
                ag(k, j, way, 0, sub).start()

    def ag_relay(k, step):
        for sub in range(2):
            for way in range(2):
                for j in range(2):
                    @pl.when(step < hops(j, way))
                    def _():
                        ag_copy(k, j, way, step, sub, 1).wait_recv()

                    @pl.when(step < hops(j, way) - 1)
                    def _():
                        ag(k, j, way, step + 1, sub).start()

    for k in range(CHUNKS):
        @pl.when(c != h)
        def _():
            exchange_wait(k, 0)
        ag_first(k, 0)

    load_pool.wait()
    TB = min(LANES, TOK)

    @pl.loop(0, TOK // TB)
    def _(blk):
        at = pl.multiple_of(blk * TB, TB)
        col = jnp.broadcast_to(idx_ref[:, pl.ds(at, TB)], (LANES, TB)).T
        lane = lax.broadcasted_iota(jnp.int32, (TB, LANES), 1)
        onehot = jnp.concatenate(
            [jnp.where(col == lane + i * LANES, 1.0, 0.0).astype(BF16) for i in range(POOL // LANES)], axis=1
        )
        picked = jnp.dot(onehot, poolv[...], preferred_element_type=F32)
        mean = jnp.mean(picked * picked, axis=1, keepdims=True)
        na[h, pl.ds(at, TB), :] = (picked * lax.rsqrt(mean + 1e-06)).astype(BF16)

    seg = x * 2 + c
    own_seg = na.at[h, pl.ds(pl.multiple_of(seg * SEG, SEG), SEG)]
    nseg = remote(own_seg, own_seg, nseg_s, nseg_r, across)
    nseg.start()

    for k in range(CHUNKS):
        exchange_wait(k, 1)
        ag_first(k, 1)

    def slice_out(d):
        q = rem(p + d, NP)
        return remote(wba.at[q], wa.at[p], wa_s.at[d], wa_r.at[d], (q, s))

    def slice_wait(d):
        q = rem(p + NP - d, NP)
        remote(wba.at[q], wa.at[q], wa_s.at[d], wa_r.at[d], (q, s)).wait_recv()

    @pl.loop(1, NP)
    def _(d):
        slice_out(d).start()

    wa[p] = wba[p]

    got_seg = na.at[1 - h, pl.ds(pl.multiple_of(seg * SEG, SEG), SEG)]

    def seg_out(d):
        g = rem(seg + d, G)
        return remote(got_seg, got_seg, nb_s.at[d], nb_r.at[d], ((g // 2 * 2 + yl) * 2 + rem(g, 2), s))

    def seg_wait(d):
        g = rem(seg + G - d, G)
        part = na.at[1 - h, pl.ds(pl.multiple_of(g * SEG, SEG), SEG)]
        remote(part, part, nb_s.at[d], nb_r.at[d], sibling).wait_recv()

    def share_segments():
        remote(got_seg, got_seg, nseg_s, nseg_r, across).wait_recv()

        @pl.loop(1, G)
        def _(d):
            seg_out(d).start()

    cot_mine = ca.at[1 - h, pl.ds(pl.multiple_of(c * HT, HT), HT)]
    cot_other = ca.at[1 - h, pl.ds(pl.multiple_of((1 - c) * HT, HT), HT)]
    cot_pass = remote(cot_mine, cot_mine, cot_fs, cot_fr, sibling)

    def pass_cotangent():
        remote(cot_mine, cot_mine, cot_s.at[0], cot_r.at[1], sibling).wait_recv()
        cot_pass.start()

    eye = lax.broadcasted_iota(jnp.int32, (NP, LANES), 0) == lax.broadcasted_iota(jnp.int32, (NP, LANES), 1)

    def part_out(d):
        q = rem(p + d, NP)
        return remote(dmine, dpart.at[p], dp_s.at[d], dp_r.at[d], (q, s))

    def part_wait(d):
        q = rem(p + NP - d, NP)
        remote(dmine, dpart.at[q], dp_s.at[d], dp_r.at[d], (q, s)).wait_recv()

    def partial_distances():
        @pl.loop(1, NP)
        def _(d):
            slice_wait(d)

        d1[...] = jnp.zeros_like(d1)

        @pl.loop(0, NP)
        def _(i):
            own = wa[i].astype(F32)
            for ahead in range(1, NP // 2 + 1):
                j = rem(i + ahead, NP)
                off = own - wa[j].astype(F32)
                squares = jnp.sum(off * off, axis=0, keepdims=True)
                d1[i, pl.ds(j, 1), :] = squares
                d1[j, pl.ds(i, 1), :] = squares

    def send_distances():
        flat = d1[...].reshape(NP * NP, LANES)
        spread = jnp.dot(flat, jnp.ones((LANES, LANES), F32), precision=HIGHEST, preferred_element_type=F32)
        for i in range(NP):
            dmine[i:i + 1, :] = jnp.sum(
                jnp.where(eye, spread[i * NP:(i + 1) * NP, :], 0.0), axis=0, keepdims=True
            )

        @pl.loop(1, NP)
        def _(d):
            part_out(d).start()

    BITS = NS.bit_length() - 1

    def pair_out(bit):
        mask = 1 << bit
        low = rem(s // mask, 2)
        return remote(dpair.at[bit, 0], dpair.at[bit, 1], dh_s.at[bit], dh_r.at[bit], (p, s + mask - 2 * mask * low))

    def sum_distances(bit):
        if bit == 0:
            dpart[p] = dmine[...]

            @pl.loop(1, NP)
            def _(d):
                part_wait(d)

            total = jnp.sum(dpart[...], axis=0)
        else:
            pair_out(bit - 1).wait_recv()
            total = dpair[bit - 1, 0] + dpair[bit - 1, 1]
        dpair[bit, 0] = total
        if bit < BITS:
            pair_out(bit).start()

    inverse_band = 1.0 / jnp.full((1, LANES), scale_ref[0], jnp.int32).astype(F32)
    repulse = 2.0 * inverse_band

    def kernel_matrix():
        near = jnp.exp(-dpair[BITS, 0] * inverse_band)
        for i in range(NP):
            d1[i] = jnp.where(eye, jnp.broadcast_to(near[i:i + 1, :], (NP, LANES)), 0.0)
        flat = d1[...].reshape(NP * NP, LANES)
        spread = jnp.dot(flat, jnp.ones((LANES, LANES), F32), precision=HIGHEST, preferred_element_type=F32)
        krep[...] = spread.reshape(NP, NP, LANES)

    def turn(source, target, hb, at):
        target[:, pl.ds(pl.multiple_of(hb * TOK + at, HT), HT)] = source[hb, pl.ds(at, HT), :].T

    def hidden(k, blk, flip):
        hb = rem(h + blk // 2, 2)
        at = pl.multiple_of(rem(blk, 2) * HT, HT)
        normed = na[hb, pl.ds(at, HT), :]
        upstream = ca[hb, pl.ds(at, HT), :]
        rows = pl.multiple_of(hb * TOK + at, HT)
        up_proj = jnp.dot(normed, wg[k, 0], preferred_element_type=F32) * D ** (-0.5)
        back_proj = jnp.dot(upstream, wg[k, 1], preferred_element_type=F32) * FF ** (-0.5)
        act_full, gelu_slope = gelu_pair(up_proj)
        act[k, pl.ds(rows, HT), :] = act_full.astype(BF16)
        upg[k, pl.ds(rows, HT), :] = (back_proj * gelu_slope).astype(BF16)
        if flip:
            @pl.when(blk >= 2)
            def _():
                turn(na, nt, hb, at)
                turn(ca, ct, hb, at)

    def gradient(k, j, b):
        lhs = (nt if j == 0 else ct)[pl.ds(pl.multiple_of(b * 2 * RB, 2 * RB), 2 * RB), :]
        return jnp.dot(lhs, (upg if j == 0 else act)[k], preferred_element_type=F32)

    def rs(k, j, way, step, sub):
        n = slot(k, j, way, step, sub)
        return remote(rss.at[n], rsr.at[n], rs_s.at[n], rs_r.at[n], zdev[way])

    def rs_part(k, j, way, step, first):
        left = hops(j, way) - step
        part = gradient(k, j, rem(z + left, NZ) if way == 0 else rem(z + NZ - left, NZ))
        for sub in range(2):
            total = part[sub * RB:(sub + 1) * RB, :]
            n = slot(k, j, way, step, sub)
            if not first:
                rs(k, j, way, step - 1, sub).wait_recv()
                total = total + rsr[n - 2].astype(F32)
            rss[n] = total.astype(BF16)
            rs(k, j, way, step, sub).start()

    def rs_step(k, step, first=False):
        for way in range(2):
            for j in range(2):
                @pl.when(step < hops(j, way))
                def _():
                    rs_part(k, j, way, step, first)

    grad_scale = 1.0 / (TOK * NZ * 2 * D)

    def score_out(k, o, sub):
        return remote(sc.at[k, sub, o], sa.at[k, role], sa_s.at[k * NP + o * 2 + sub], sa_r.at[k * NP + role],
                      (o * 2 + c, z * 2 + sub))

    def rs_final(k):
        parts = [gradient(k, j, z) for j in range(2)]
        for sub in range(2):
            for j in range(2):
                total = parts[j][sub * RB:(sub + 1) * RB, :]
                for way in range(2):
                    rs(k, j, way, hops(j, way) - 1, sub).wait_recv()
                    total = total + rsr[slot(k, j, way, hops(j, way) - 1, sub)].astype(F32)
                factor = (D if j == 0 else FF) ** (-0.5) * grad_scale
                score = (total * -factor).astype(BF16)
                for tile in range(TC):
                    sc[k, sub, tile * 2 + j] = score[:, tile * LANES:(tile + 1) * LANES]
                for n in range(TC):
                    o = rem(xy // 2 + n, TC) * 2 + j

                    @pl.when(o * 2 + sub != role)
                    def _():
                        score_out(k, o, sub).start()

        sa[k, role] = sc[k, h, xy]

    def transport_out(k, d):
        q = rem(p + d, NP)
        return remote(tr.at[k, q], ta.at[k, p], ta_s.at[k * NP + d], ta_r.at[k * NP + d], (q, s))

    def transport_wait(k, d):
        q = rem(p + NP - d, NP)
        remote(tr.at[k, 0], ta.at[k, q], ta_s.at[k * NP + d], ta_r.at[k * NP + d], sibling).wait_recv()

    params_total = 2 * D * FF

    def move(k):
        for q in range(NP):
            @pl.when(q != role)
            def _():
                remote(sc.at[k, 0, 0], sa.at[k, q], sa_s.at[0], sa_r.at[k * NP + q], sibling).wait_recv()

            fld[q] = sa[k, q].astype(F32) - repulse * wa[q, k * RB:(k + 1) * RB, :].astype(F32)

        @pl.loop(1, NP + 1)
        def _(d):
            i = rem(p + d, NP)
            weighted = krep[i, 0:1, :] * fld[0]
            for j in range(1, NP):
                weighted = weighted + krep[i, j:j + 1, :] * fld[j]
            kernel_total = jnp.sum(krep[i], axis=0, keepdims=True)
            own_w = wa[i, k * RB:(k + 1) * RB, :].astype(F32)
            tr[k, i] = (params_total / NP * (weighted + repulse * kernel_total * own_w)).astype(BF16)

            @pl.when(d < NP)
            def _():
                transport_out(k, d).start()

        ta[k, p] = tr[k, p]

    def collect(k):
        @pl.loop(1, NP)
        def _(d):
            transport_wait(k, d)

        out_ref[k] = ta[k]

    ag_relay(0, 0)
    for half in range(2):
        turn(na, nt, h, half * HT)
    ag_relay(0, 1)
    share_segments()

    @pl.when(c == h)
    def _():
        cot_load.wait()

    @pl.when(c != h)
    def _():
        remote(cot_hbm, ca.at[h], cot_s.at[0], cot_r.at[0], sibling).wait_recv()

    for half in range(2):
        turn(ca, ct, h, half * HT)
    ag_relay(0, 2)
    partial_distances()
    ag_relay(1, 0)
    send_distances()
    ag_relay(0, 3)
    pass_cotangent()

    @pl.loop(0, 4)
    def _(blk):
        @pl.when(blk == 2)
        def _():
            @pl.loop(1, G)
            def _(d):
                seg_wait(d)

            remote(cot_other, cot_other, cot_fs, cot_fr, sibling).wait_recv()

        hidden(0, blk, True)

        @pl.when(blk < 3)
        def _():
            ag_relay(1, blk + 1)

        for bit in range(2):
            @pl.when(blk == bit + 2)
            def _():
                sum_distances(bit)

    rs_step(0, 0, True)

    @pl.loop(0, 4)
    def _(blk):
        hidden(1, blk, False)

        @pl.when(blk < 3)
        def _():
            rs_step(0, blk + 1)

        for bit in range(2, BITS + 1):
            @pl.when(blk == bit - 2)
            def _():
                sum_distances(bit)

    rs_step(1, 0, True)
    rs_final(0)
    kernel_matrix()
    rs_step(1, 1)
    rs_step(1, 2)
    move(0)
    rs_step(1, 3)
    collect(0)
    rs_final(1)
    move(1)
    collect(1)

    @pl.when(c == h)
    def _():
        for k in range(CHUNKS):
            exchange(k, 1 - c, sibling).wait_send()
        cot_full.wait_send()

    @pl.when(c != h)
    def _():
        for k in range(CHUNKS):
            for half in range(2):
                exchange(k, half, (xy * 2 + half, z * 2 + 1 - h)).wait_send()
        for half in range(2):
            cot_half(half).wait_send()

    nseg.wait_send()
    cot_pass.wait_send()
    for bit in range(BITS):
        pair_out(bit).wait_send()

    @pl.loop(1, G)
    def _(d):
        seg_out(d).wait_send()

    @pl.loop(1, NP)
    def _(d):
        slice_out(d).wait_send()
        part_out(d).wait_send()
        for k in range(CHUNKS):
            transport_out(k, d).wait_send()

    for k in range(CHUNKS):
        for o in range(NXY):
            for sub in range(2):
                @pl.when(o * 2 + sub != role)
                def _():
                    score_out(k, o, sub).wait_send()

    for k in range(CHUNKS):
        for j in range(2):
            for way in range(2):
                @pl.loop(0, hops(j, way))
                def _(step):
                    for sub in range(2):
                        ag(k, j, way, step, sub).wait_send()
                        rs(k, j, way, step, sub).wait_send()


def stein_transport(NP, NS, kernel_scale, batch_index, flat_w, pool, cotangent):
    NZ = NS // 2
    TOK, D = cotangent.shape
    RB = D // NS
    FF = flat_w.shape[0] * LANES // RB // 2
    POOL = pool.shape[0]
    NXY, G = NP // 2, NP // 2
    TC = FF // LANES // 2 // CHUNKS
    CH = TC * LANES
    assert TC * 2 == NXY
    dma = pltpu.SemaphoreType.DMA
    ring = CHUNKS * 2 * 2 * (NZ // 2) * 2
    scratch = [
        pltpu.VMEM(flat_w.shape, F32),
        pltpu.VMEM((POOL, D), BF16),
        pltpu.VMEM((2, CHUNKS, 2, RB, CH), BF16),
        pltpu.VMEM((NP, CHUNKS * RB, LANES), BF16),
        pltpu.VMEM((CHUNKS, 2, D, CH), BF16),
        pltpu.VMEM((2, TOK, D), BF16),
        pltpu.VMEM((2, TOK, D), BF16),
        pltpu.VMEM((D, 2 * TOK), BF16),
        pltpu.VMEM((D, 2 * TOK), BF16),
        pltpu.VMEM((CHUNKS, 2 * TOK, CH), BF16),
        pltpu.VMEM((CHUNKS, 2 * TOK, CH), BF16),
        pltpu.VMEM((ring, RB, CH), BF16),
        pltpu.VMEM((ring, RB, CH), BF16),
        pltpu.VMEM((CHUNKS, 2, NXY, RB, LANES), BF16),
        pltpu.VMEM((CHUNKS, NP, RB, LANES), BF16),
        pltpu.VMEM((NP, CHUNKS * RB, LANES), BF16),
        pltpu.VMEM((NP, RB, LANES), F32),
        pltpu.VMEM((CHUNKS, NP, RB, LANES), BF16),
        pltpu.VMEM((CHUNKS, NP, RB, LANES), BF16),
        pltpu.VMEM((NP, NP, LANES), F32),
        pltpu.VMEM((NP, LANES), F32),
        pltpu.VMEM((NP, NP, LANES), F32),
        pltpu.VMEM((NS.bit_length(), 2, NP, LANES), F32),
        pltpu.VMEM((NP, NP, LANES), F32),
        dma((3,)),
        dma((2 * CHUNKS,)), dma((2 * CHUNKS,)),
        dma((2,)), dma((2,)), dma(()), dma(()),
        dma(()), dma(()), dma((G,)), dma((G,)),
        dma((NP,)), dma((NP,)),
        dma((ring,)), dma((ring,)), dma((ring,)), dma((ring,)),
        dma((NP,)), dma((NP,)), dma((NS.bit_length(),)), dma((NS.bit_length(),)),
        dma((CHUNKS * NP,)), dma((CHUNKS * NP,)), dma((CHUNKS * NP,)), dma((CHUNKS * NP,)),
    ]
    anywhere = pl.BlockSpec(memory_space=pl.ANY)
    vmem = pl.BlockSpec(memory_space=pltpu.VMEM)
    return pl.pallas_call(
        functools.partial(stein_kernel, (NP, NS, RB, TOK, D, FF, POOL)),
        out_shape=jax.ShapeDtypeStruct((CHUNKS, NP, RB, LANES), BF16),
        in_specs=[pl.BlockSpec(memory_space=pltpu.SMEM), vmem, anywhere, anywhere, anywhere],
        out_specs=vmem,
        scratch_shapes=scratch,
        compiler_params=pltpu.CompilerParams(
            collective_id=0, has_side_effects=True, vmem_limit_bytes=62 * 1024 * 1024
        ),
        name="stein",
    )(kernel_scale, batch_index.reshape(1, TOK), flat_w, pool, cotangent)


def adam_kernel(NT, moved_ref, w_ref, m_ref, v_ref, new_w, new_m, new_v, transport_ref):
    NP, rows = moved_ref.shape[1:3]
    TC = NT // 2 // CHUNKS
    for k in range(CHUNKS):
        for q in range(NP):
            o, half = q // 2, q % 2
            t = (half * CHUNKS + k) * TC + o // 2
            transport_ref[pl.ds(2 * t + o % 2, rows, stride=2 * NT), :] = moved_ref[k, q].astype(F32)
    transport = transport_ref[...]
    new_first = 0.9 * m_ref[...] - 0.1 * transport
    new_second = 0.999 * v_ref[...] + 0.001 * transport * transport
    new_m[...] = new_first
    new_v[...] = new_second
    new_w[...] = w_ref[...] - 0.01 * new_first / (jnp.sqrt(new_second) + 1e-08)


def adam(moved, flat_w, flat_m, flat_v):
    chunks, NP, RB, lanes = moved.shape
    steps = RB // 16
    size = flat_w.shape[0] // steps
    block = pl.BlockSpec((size, lanes), lambda i: (i, 0))
    shape = jax.ShapeDtypeStruct(flat_w.shape, F32)
    return pl.pallas_call(
        functools.partial(adam_kernel, flat_w.shape[0] // RB // 2),
        out_shape=(shape,) * 4,
        grid=(steps,),
        in_specs=[pl.BlockSpec((chunks, NP, 16, lanes), lambda i: (0, 0, i, 0)), block, block, block],
        out_specs=(block,) * 4,
        name="adam",
    )(moved, flat_w, flat_m, flat_v)


def local(NP, NS, pool, batch_index, kernel_scale, cotangent, weights, first_moment, second_moment):
    rows, pair, hidden_units = weights.shape[1:]

    def flatten(a):
        return a.reshape(rows, pair, hidden_units // LANES, LANES).transpose(0, 2, 1, 3).reshape(-1, LANES)

    def unflatten(a):
        a = a.reshape(rows, hidden_units // LANES, pair, LANES).transpose(0, 2, 1, 3)
        return a.reshape(1, rows, pair, hidden_units)

    flat_w = flatten(weights[0])
    moved = stein_transport(NP, NS, kernel_scale, batch_index, flat_w, pool, cotangent[0])
    outs = adam(moved, flat_w, flatten(first_moment[0]), flatten(second_moment[0]))
    return tuple(unflatten(a) for a in outs)


def solution(mesh):
    placed = (
        P("shard", None),
        P("shard"),
        P(),
        P("particle", "shard", None),
        P("particle", "shard", None, None),
        P("particle", "shard", None, None),
        P("particle", "shard", None, None),
    )
    return jax.shard_map(
        functools.partial(local, mesh.shape["particle"], mesh.shape["shard"]),
        mesh=mesh,
        in_specs=placed,
        out_specs=(P("particle", "shard", None, None),) * 4,
        check_vma=False,
    )
```

```python
import functools

import jax
import jax.numpy as jnp
from jax import lax
from jax.experimental import pallas as pl
from jax.experimental.pallas import tpu as pltpu
from jax.sharding import PartitionSpec as P

MESH = pl.DeviceIdType.MESH
CHUNKS = 2
LANES = 128
HIGHEST = lax.Precision.HIGHEST
F32 = jnp.float32
BF16 = jnp.bfloat16


def gelu_pair(up_proj):
    cdf_part = 0.5 * (1.0 + lax.erf(up_proj * 0.7071067811865476))
    density = jnp.exp(-0.5 * up_proj * up_proj) * 0.3989422804014327
    return (up_proj * cdf_part, cdf_part + up_proj * density)


def remote(src, dst, send_sem, recv_sem, device):
    return pltpu.make_async_remote_copy(
        src_ref=src,
        dst_ref=dst,
        send_sem=send_sem,
        recv_sem=recv_sem,
        device_id=device,
        device_id_type=MESH,
    )


def stein_kernel(
    dims,
    scale_ref, idx_ref, w_hbm, pool_hbm, cot_hbm,
    out_ref,
    wf, poolv, wbr, wba, wg, na, ca, nt, ct, act, upg, rss, rsr, sc, sa, wa, fld, tr, ta,
    d1, dmine, dpart, dpair, krep,
    load_sem, ex_s, ex_r, cot_s, cot_r, cot_fs, cot_fr, nseg_s, nseg_r, nb_s, nb_r,
    wa_s, wa_r, ag_s, ag_r, rs_s, rs_r, dp_s, dp_r, dh_s, dh_r, sa_s, sa_r, ta_s, ta_r,
):
    NP, NS, RB, TOK, D, FF, POOL = dims
    NZ = NS // 2
    NXY, NX = NP // 2, NP // 4
    G = NX * 2
    NT = FF // LANES
    TC = NT // 2 // CHUNKS
    CH = TC * LANES
    SEG = TOK // G
    HT = TOK // 2
    rem = lax.rem
    p, s = lax.axis_index("particle"), lax.axis_index("shard")
    c, xy = rem(p, 2), p // 2
    x, yl = xy // 2, rem(xy, 2)
    h, z = rem(s, 2), s // 2
    zdev = (
        (p, rem(z + 1, NZ) * 2 + h),
        (p, rem(z + NZ - 1, NZ) * 2 + h),
    )
    sibling = (xy * 2 + 1 - c, s)
    across = (p, z * 2 + 1 - h)
    diagonal = (xy * 2 + 1 - c, z * 2 + 1 - h)
    role = xy * 2 + h

    load_w = pltpu.make_async_copy(w_hbm, wf, load_sem.at[0])
    load_w.start()
    load_pool = pltpu.make_async_copy(pool_hbm, poolv, load_sem.at[1])
    load_pool.start()
    barrier = pltpu.get_barrier_semaphore()

    def greet(device):
        pl.semaphore_signal(barrier, inc=1, device_id=device, device_id_type=MESH)

    greet(zdev[0])
    greet(zdev[1])
    greet(diagonal)
    for bit in range(1, NZ.bit_length() - 1):
        greet((p, s + (2 << bit) - (4 << bit) * rem(z // (1 << bit), 2)))

    @pl.loop(1, NP)
    def _(d):
        greet((rem(p + d, NP), s))

    @pl.loop(0, NXY)
    def _(o):
        greet((o * 2 + c, z * 2 + 1 - h))

    load_w.wait()
    for half in range(2):
        for k in range(CHUNKS):
            for tile in range(TC):
                for j in range(2):
                    t = (half * CHUNKS + k) * TC + tile
                    v = wf[pl.ds(2 * t + j, RB, stride=2 * NT), :].astype(BF16)
                    wbr[half, k, j, :, tile * LANES:(tile + 1) * LANES] = v
                    wba[(tile * 2 + j) * 2 + half, k * RB:(k + 1) * RB, :] = v
    pl.semaphore_wait(barrier, NP + NXY + NZ.bit_length())

    own_rows = pl.ds(pl.multiple_of((z * 2 + h) * RB, RB), RB)
    sub_at_dest = rem(h + c, 2)

    def exchange(k, half, device):
        return remote(
            wbr.at[half, k], wg.at[k, :, own_rows, :],
            ex_s.at[k * 2 + half], ex_r.at[k * 2 + sub_at_dest], device,
        )

    def cot_half(half):
        part = cot_hbm.at[pl.ds(half * HT, HT)]
        return remote(part, ca.at[h, pl.ds(half * HT, HT)], cot_s.at[half], cot_r.at[1],
                      (xy * 2 + half, z * 2 + 1 - h))

    cot_load = pltpu.make_async_copy(cot_hbm, ca.at[h], load_sem.at[2])
    cot_full = remote(cot_hbm, ca.at[h], cot_s.at[0], cot_r.at[0], sibling)

    @pl.when(c == h)
    def _():
        for k in range(CHUNKS):
            exchange(k, 1 - c, sibling).start()
        for k in range(CHUNKS):
            wg[k, :, own_rows, :] = wbr[c, k]
        cot_load.start()
        cot_full.start()

    @pl.when(c != h)
    def _():
        for k in range(CHUNKS):
            for half in range(2):
                exchange(k, half, (xy * 2 + half, z * 2 + 1 - h)).start()
        for half in range(2):
            cot_half(half).start()

    def exchange_wait(k, sub):
        rows = pl.ds(pl.multiple_of((z * 2 + rem(h + sub, 2)) * RB, RB), RB)
        remote(wbr.at[0, k], wg.at[k, :, rows, :], ex_s.at[0], ex_r.at[k * 2 + sub], sibling).wait_recv()

    FAR = NZ // 2

    def hops(j, way):
        return FAR if j == way else NZ - 1 - FAR

    def slot(k, j, way, step, sub):
        return (((k * 2 + j) * 2 + way) * FAR + step) * 2 + sub

    def ag_copy(k, j, way, step, sub, back):
        b = rem(z + 2 * NZ - step - back, NZ) if way == 0 else rem(z + step + back, NZ)
        rows = pl.ds(pl.multiple_of((b * 2 + rem(h + sub, 2)) * RB, RB), RB)
        n = slot(k, j, way, step, sub)
        return remote(wg.at[k, j, rows, :], wg.at[k, j, rows, :], ag_s.at[n], ag_r.at[n], zdev[way])

    def ag(k, j, way, step, sub):
        return ag_copy(k, j, way, step, sub, 0)

    def ag_first(k, sub):
        for way in range(2):
            for j in range(2):
                ag(k, j, way, 0, sub).start()

    def ag_relay(k, step):
        for sub in range(2):
            for way in range(2):
                for j in range(2):
                    @pl.when(step < hops(j, way))
                    def _():
                        ag_copy(k, j, way, step, sub, 1).wait_recv()

                    @pl.when(step < hops(j, way) - 1)
                    def _():
                        ag(k, j, way, step + 1, sub).start()

    for k in range(CHUNKS):
        @pl.when(c != h)
        def _():
            exchange_wait(k, 0)
        ag_first(k, 0)

    load_pool.wait()
    TB = min(LANES, TOK)

    @pl.loop(0, TOK // TB)
    def _(blk):
        at = pl.multiple_of(blk * TB, TB)
        col = jnp.broadcast_to(idx_ref[:, pl.ds(at, TB)], (LANES, TB)).T
        lane = lax.broadcasted_iota(jnp.int32, (TB, LANES), 1)
        onehot = jnp.concatenate(
            [jnp.where(col == lane + i * LANES, 1.0, 0.0).astype(BF16) for i in range(POOL // LANES)], axis=1
        )
        picked = jnp.dot(onehot, poolv[...], preferred_element_type=F32)
        mean = jnp.mean(picked * picked, axis=1, keepdims=True)
        na[h, pl.ds(at, TB), :] = (picked * lax.rsqrt(mean + 1e-06)).astype(BF16)

    seg = x * 2 + c
    own_seg = na.at[h, pl.ds(pl.multiple_of(seg * SEG, SEG), SEG)]
    nseg = remote(own_seg, own_seg, nseg_s, nseg_r, across)
    nseg.start()

    for k in range(CHUNKS):
        exchange_wait(k, 1)
        ag_first(k, 1)

    def slice_out(d):
        q = rem(p + d, NP)
        return remote(wba.at[q], wa.at[p], wa_s.at[d], wa_r.at[d], (q, s))

    def slice_wait(d):
        q = rem(p + NP - d, NP)
        remote(wba.at[q], wa.at[q], wa_s.at[d], wa_r.at[d], (q, s)).wait_recv()

    def send_slices():
        @pl.loop(1, NP)
        def _(d):
            slice_out(d).start()

        wa[p] = wba[p]

    got_seg = na.at[1 - h, pl.ds(pl.multiple_of(seg * SEG, SEG), SEG)]

    def seg_out(d):
        g = rem(seg + d, G)
        return remote(got_seg, got_seg, nb_s.at[d], nb_r.at[d], ((g // 2 * 2 + yl) * 2 + rem(g, 2), s))

    def seg_wait(d):
        g = rem(seg + G - d, G)
        part = na.at[1 - h, pl.ds(pl.multiple_of(g * SEG, SEG), SEG)]
        remote(part, part, nb_s.at[d], nb_r.at[d], sibling).wait_recv()

    def share_segments():
        remote(got_seg, got_seg, nseg_s, nseg_r, across).wait_recv()

        @pl.loop(1, G)
        def _(d):
            seg_out(d).start()

    cot_mine = ca.at[1 - h, pl.ds(pl.multiple_of(c * HT, HT), HT)]
    cot_other = ca.at[1 - h, pl.ds(pl.multiple_of((1 - c) * HT, HT), HT)]
    cot_pass = remote(cot_mine, cot_mine, cot_fs, cot_fr, sibling)

    def pass_cotangent():
        remote(cot_mine, cot_mine, cot_s.at[0], cot_r.at[1], sibling).wait_recv()
        cot_pass.start()

    eye = lax.broadcasted_iota(jnp.int32, (NP, LANES), 0) == lax.broadcasted_iota(jnp.int32, (NP, LANES), 1)

    def part_out(d):
        q = rem(p + d, NP)
        return remote(dmine, dpart.at[p], dp_s.at[d], dp_r.at[d], (q, s))

    def part_wait(d):
        q = rem(p + NP - d, NP)
        remote(dmine, dpart.at[q], dp_s.at[d], dp_r.at[d], (q, s)).wait_recv()

    def partial_distances():
        @pl.loop(1, NP)
        def _(d):
            slice_wait(d)

        d1[...] = jnp.zeros_like(d1)

        @pl.loop(0, NP)
        def _(i):
            own = wa[i].astype(F32)
            for ahead in range(1, NP // 2 + 1):
                j = rem(i + ahead, NP)
                off = own - wa[j].astype(F32)
                squares = jnp.sum(off * off, axis=0, keepdims=True)
                d1[i, pl.ds(j, 1), :] = squares
                d1[j, pl.ds(i, 1), :] = squares

    def send_distances():
        flat = d1[...].reshape(NP * NP, LANES)
        spread = jnp.dot(flat, jnp.ones((LANES, LANES), F32), precision=HIGHEST, preferred_element_type=F32)
        for i in range(NP):
            dmine[i:i + 1, :] = jnp.sum(
                jnp.where(eye, spread[i * NP:(i + 1) * NP, :], 0.0), axis=0, keepdims=True
            )

        @pl.loop(1, NP)
        def _(d):
            part_out(d).start()

    BITS = NS.bit_length() - 1

    def pair_out(bit):
        mask = 1 << bit
        low = rem(s // mask, 2)
        return remote(dpair.at[bit, 0], dpair.at[bit, 1], dh_s.at[bit], dh_r.at[bit], (p, s + mask - 2 * mask * low))

    def sum_distances(bit):
        if bit == 0:
            dpart[p] = dmine[...]

            @pl.loop(1, NP)
            def _(d):
                part_wait(d)

            total = jnp.sum(dpart[...], axis=0)
        else:
            pair_out(bit - 1).wait_recv()
            total = dpair[bit - 1, 0] + dpair[bit - 1, 1]
        dpair[bit, 0] = total
        if bit < BITS:
            pair_out(bit).start()

    inverse_band = 1.0 / jnp.full((1, LANES), scale_ref[0], jnp.int32).astype(F32)
    repulse = 2.0 * inverse_band

    def kernel_matrix():
        near = jnp.exp(-dpair[BITS, 0] * inverse_band)
        for i in range(NP):
            d1[i] = jnp.where(eye, jnp.broadcast_to(near[i:i + 1, :], (NP, LANES)), 0.0)
        flat = d1[...].reshape(NP * NP, LANES)
        spread = jnp.dot(flat, jnp.ones((LANES, LANES), F32), precision=HIGHEST, preferred_element_type=F32)
        krep[...] = spread.reshape(NP, NP, LANES)

    def turn(source, target, hb, at):
        target[:, pl.ds(pl.multiple_of(hb * TOK + at, HT), HT)] = source[hb, pl.ds(at, HT), :].T

    def hidden(k, blk, flip):
        hb = rem(h + blk // 2, 2)
        at = pl.multiple_of(rem(blk, 2) * HT, HT)
        normed = na[hb, pl.ds(at, HT), :]
        upstream = ca[hb, pl.ds(at, HT), :]
        rows = pl.multiple_of(hb * TOK + at, HT)
        up_proj = jnp.dot(normed, wg[k, 0], preferred_element_type=F32) * D ** (-0.5)
        back_proj = jnp.dot(upstream, wg[k, 1], preferred_element_type=F32) * FF ** (-0.5)
        act_full, gelu_slope = gelu_pair(up_proj)
        act[k, pl.ds(rows, HT), :] = act_full.astype(BF16)
        upg[k, pl.ds(rows, HT), :] = (back_proj * gelu_slope).astype(BF16)
        if flip:
            @pl.when(blk >= 2)
            def _():
                turn(na, nt, hb, at)
                turn(ca, ct, hb, at)

    def gradient(k, j, b):
        lhs = (nt if j == 0 else ct)[pl.ds(pl.multiple_of(b * 2 * RB, 2 * RB), 2 * RB), :]
        return jnp.dot(lhs, (upg if j == 0 else act)[k], preferred_element_type=F32)

    def rs(k, j, way, step, sub):
        n = slot(k, j, way, step, sub)
        return remote(rss.at[n], rsr.at[n], rs_s.at[n], rs_r.at[n], zdev[way])

    def rs_part(k, j, way, step, first):
        left = hops(j, way) - step
        part = gradient(k, j, rem(z + left, NZ) if way == 0 else rem(z + NZ - left, NZ))
        for sub in range(2):
            total = part[sub * RB:(sub + 1) * RB, :]
            n = slot(k, j, way, step, sub)
            if not first:
                rs(k, j, way, step - 1, sub).wait_recv()
                total = total + rsr[n - 2].astype(F32)
            rss[n] = total.astype(BF16)
            rs(k, j, way, step, sub).start()

    def rs_step(k, step, first=False):
        for way in range(2):
            for j in range(2):
                @pl.when(step < hops(j, way))
                def _():
                    rs_part(k, j, way, step, first)

    grad_scale = 1.0 / (TOK * NZ * 2 * D)

    def score_out(k, o, sub):
        return remote(sc.at[k, sub, o], sa.at[k, role], sa_s.at[k * NP + o * 2 + sub], sa_r.at[k * NP + role],
                      (o * 2 + c, z * 2 + sub))

    def rs_final(k):
        parts = [gradient(k, j, z) for j in range(2)]
        for sub in range(2):
            for j in range(2):
                total = parts[j][sub * RB:(sub + 1) * RB, :]
                for way in range(2):
                    rs(k, j, way, hops(j, way) - 1, sub).wait_recv()
                    total = total + rsr[slot(k, j, way, hops(j, way) - 1, sub)].astype(F32)
                factor = (D if j == 0 else FF) ** (-0.5) * grad_scale
                score = (total * -factor).astype(BF16)
                for tile in range(TC):
                    sc[k, sub, tile * 2 + j] = score[:, tile * LANES:(tile + 1) * LANES]
                for n in range(TC):
                    o = rem(xy // 2 + n, TC) * 2 + j

                    @pl.when(o * 2 + sub != role)
                    def _():
                        score_out(k, o, sub).start()

        sa[k, role] = sc[k, h, xy]

    def transport_out(k, d):
        q = rem(p + d, NP)
        return remote(tr.at[k, q], ta.at[k, p], ta_s.at[k * NP + d], ta_r.at[k * NP + d], (q, s))

    def transport_wait(k, d):
        q = rem(p + NP - d, NP)
        remote(tr.at[k, 0], ta.at[k, q], ta_s.at[k * NP + d], ta_r.at[k * NP + d], sibling).wait_recv()

    params_total = 2 * D * FF

    def move(k):
        for q in range(NP):
            @pl.when(q != role)
            def _():
                remote(sc.at[k, 0, 0], sa.at[k, q], sa_s.at[0], sa_r.at[k * NP + q], sibling).wait_recv()

            fld[q] = sa[k, q].astype(F32) - repulse * wa[q, k * RB:(k + 1) * RB, :].astype(F32)

        @pl.loop(1, NP + 1)
        def _(d):
            i = rem(p + d, NP)
            weighted = krep[i, 0:1, :] * fld[0]
            for j in range(1, NP):
                weighted = weighted + krep[i, j:j + 1, :] * fld[j]
            kernel_total = jnp.sum(krep[i], axis=0, keepdims=True)
            own_w = wa[i, k * RB:(k + 1) * RB, :].astype(F32)
            tr[k, i] = (params_total / NP * (weighted + repulse * kernel_total * own_w)).astype(BF16)

            @pl.when(d < NP)
            def _():
                transport_out(k, d).start()

        ta[k, p] = tr[k, p]

    def collect(k):
        @pl.loop(1, NP)
        def _(d):
            transport_wait(k, d)

        out_ref[k] = ta[k]

    def drain_gather():
        @pl.when(c == h)
        def _():
            for k in range(CHUNKS):
                exchange(k, 1 - c, sibling).wait_send()
            cot_full.wait_send()

        @pl.when(c != h)
        def _():
            for k in range(CHUNKS):
                for half in range(2):
                    exchange(k, half, (xy * 2 + half, z * 2 + 1 - h)).wait_send()
            for half in range(2):
                cot_half(half).wait_send()

        nseg.wait_send()
        cot_pass.wait_send()

        @pl.loop(1, G)
        def _(d):
            seg_out(d).wait_send()

        @pl.loop(1, NP)
        def _(d):
            slice_out(d).wait_send()
            part_out(d).wait_send()

        for k in range(CHUNKS):
            for j in range(2):
                for way in range(2):
                    @pl.loop(0, hops(j, way))
                    def _(step):
                        for sub in range(2):
                            ag(k, j, way, step, sub).wait_send()

    def drain_ring():
        for bit in range(BITS):
            pair_out(bit).wait_send()

        for k in range(CHUNKS):
            for j in range(2):
                for way in range(2):
                    @pl.loop(0, hops(j, way))
                    def _(step):
                        for sub in range(2):
                            rs(k, j, way, step, sub).wait_send()

    def drain_scores():
        for k in range(CHUNKS):
            for o in range(NXY):
                for sub in range(2):
                    @pl.when(o * 2 + sub != role)
                    def _():
                        score_out(k, o, sub).wait_send()

    def drain_transport():
        @pl.loop(1, NP)
        def _(d):
            for k in range(CHUNKS):
                transport_out(k, d).wait_send()

    ag_relay(0, 0)
    for half in range(2):
        turn(na, nt, h, half * HT)
    ag_relay(0, 1)
    share_segments()
    send_slices()

    @pl.when(c == h)
    def _():
        cot_load.wait()

    @pl.when(c != h)
    def _():
        remote(cot_hbm, ca.at[h], cot_s.at[0], cot_r.at[0], sibling).wait_recv()

    for half in range(2):
        turn(ca, ct, h, half * HT)
    ag_relay(0, 2)
    ag_relay(1, 0)
    ag_relay(0, 3)
    pass_cotangent()

    @pl.loop(0, 4)
    def _(blk):
        @pl.when(blk == 2)
        def _():
            @pl.loop(1, G)
            def _(d):
                seg_wait(d)

            remote(cot_other, cot_other, cot_fs, cot_fr, sibling).wait_recv()

        hidden(0, blk, True)

        @pl.when(blk < 2)
        def _():
            ag_relay(1, blk + 1)

    rs_step(0, 0, True)
    ag_relay(1, 3)

    @pl.loop(0, 4)
    def _(blk):
        hidden(1, blk, False)

        @pl.when(blk < 3)
        def _():
            rs_step(0, blk + 1)

        @pl.when(blk == 0)
        def _():
            partial_distances()
            send_distances()

        for bit in range(2):
            @pl.when(blk == bit + 2)
            def _():
                sum_distances(bit)

    rs_step(1, 0, True)
    rs_final(0)
    sum_distances(2)
    drain_gather()
    rs_step(1, 1)
    for bit in range(3, BITS):
        sum_distances(bit)
    rs_step(1, 2)
    sum_distances(BITS)
    kernel_matrix()
    rs_step(1, 3)
    move(0)
    drain_ring()
    collect(0)
    rs_final(1)
    move(1)
    drain_scores()
    collect(1)
    drain_transport()


def stein_transport(NP, NS, kernel_scale, batch_index, flat_w, pool, cotangent):
    NZ = NS // 2
    TOK, D = cotangent.shape
    RB = D // NS
    FF = flat_w.shape[0] * LANES // RB // 2
    POOL = pool.shape[0]
    NXY, G = NP // 2, NP // 2
    TC = FF // LANES // 2 // CHUNKS
    CH = TC * LANES
    assert TC * 2 == NXY
    dma = pltpu.SemaphoreType.DMA
    ring = CHUNKS * 2 * 2 * (NZ // 2) * 2
    scratch = [
        pltpu.VMEM(flat_w.shape, F32),
        pltpu.VMEM((POOL, D), BF16),
        pltpu.VMEM((2, CHUNKS, 2, RB, CH), BF16),
        pltpu.VMEM((NP, CHUNKS * RB, LANES), BF16),
        pltpu.VMEM((CHUNKS, 2, D, CH), BF16),
        pltpu.VMEM((2, TOK, D), BF16),
        pltpu.VMEM((2, TOK, D), BF16),
        pltpu.VMEM((D, 2 * TOK), BF16),
        pltpu.VMEM((D, 2 * TOK), BF16),
        pltpu.VMEM((CHUNKS, 2 * TOK, CH), BF16),
        pltpu.VMEM((CHUNKS, 2 * TOK, CH), BF16),
        pltpu.VMEM((ring, RB, CH), BF16),
        pltpu.VMEM((ring, RB, CH), BF16),
        pltpu.VMEM((CHUNKS, 2, NXY, RB, LANES), BF16),
        pltpu.VMEM((CHUNKS, NP, RB, LANES), BF16),
        pltpu.VMEM((NP, CHUNKS * RB, LANES), BF16),
        pltpu.VMEM((NP, RB, LANES), F32),
        pltpu.VMEM((CHUNKS, NP, RB, LANES), BF16),
        pltpu.VMEM((CHUNKS, NP, RB, LANES), BF16),
        pltpu.VMEM((NP, NP, LANES), F32),
        pltpu.VMEM((NP, LANES), F32),
        pltpu.VMEM((NP, NP, LANES), F32),
        pltpu.VMEM((NS.bit_length(), 2, NP, LANES), F32),
        pltpu.VMEM((NP, NP, LANES), F32),
        dma((3,)),
        dma((2 * CHUNKS,)), dma((2 * CHUNKS,)),
        dma((2,)), dma((2,)), dma(()), dma(()),
        dma(()), dma(()), dma((G,)), dma((G,)),
        dma((NP,)), dma((NP,)),
        dma((ring,)), dma((ring,)), dma((ring,)), dma((ring,)),
        dma((NP,)), dma((NP,)), dma((NS.bit_length(),)), dma((NS.bit_length(),)),
        dma((CHUNKS * NP,)), dma((CHUNKS * NP,)), dma((CHUNKS * NP,)), dma((CHUNKS * NP,)),
    ]
    anywhere = pl.BlockSpec(memory_space=pltpu.HBM)
    vmem = pl.BlockSpec(memory_space=pltpu.VMEM)
    return pl.pallas_call(
        functools.partial(stein_kernel, (NP, NS, RB, TOK, D, FF, POOL)),
        out_shape=jax.ShapeDtypeStruct((CHUNKS, NP, RB, LANES), BF16),
        in_specs=[pl.BlockSpec(memory_space=pltpu.SMEM), vmem, anywhere, anywhere, anywhere],
        out_specs=vmem,
        scratch_shapes=scratch,
        compiler_params=pltpu.CompilerParams(
            collective_id=0, has_side_effects=True, vmem_limit_bytes=56 * 1024 * 1024
        ),
        name="stein",
    )(kernel_scale, batch_index.reshape(1, TOK), flat_w, pool, cotangent)


def adam_kernel(NT, parts, moved_ref, w_ref, m_ref, v_ref, new_w, new_m, new_v, transport_ref, out, sems):
    NP, rows = moved_ref.shape[1:3]
    TC = NT // 2 // CHUNKS
    part_rows = rows // parts
    size = part_rows * 2 * NT
    copies = []
    for part in range(parts):
        span = pl.ds(part * size, size)
        for k in range(CHUNKS):
            for q in range(NP):
                o, half = q // 2, q % 2
                t = (half * CHUNKS + k) * TC + o // 2
                piece = moved_ref[k, q, part * part_rows:(part + 1) * part_rows, :].astype(F32)
                out[0, pl.ds(part * size + 2 * t + o % 2, part_rows, stride=2 * NT), :] = piece
        transport = out[0, span, :]
        new_first = 0.9 * m_ref[span, :] - 0.1 * transport
        new_second = 0.999 * v_ref[span, :] + 0.001 * transport * transport
        out[1, span, :] = new_first
        out[2, span, :] = new_second
        out[3, span, :] = w_ref[span, :] - 0.01 * new_first / (jnp.sqrt(new_second) + 1e-08)
        for n, target in enumerate((transport_ref, new_m, new_v, new_w)):
            copy = pltpu.make_async_copy(out.at[n, span], target.at[span], sems.at[n, part])
            copy.start()
            copies.append(copy)
    for copy in copies:
        copy.wait()


def adam(moved, flat_w, flat_m, flat_v):
    RB, lanes = moved.shape[2:]
    parts = max(RB // 16, 1)
    shape = jax.ShapeDtypeStruct(flat_w.shape, F32)
    return pl.pallas_call(
        functools.partial(adam_kernel, flat_w.shape[0] // RB // 2, parts),
        out_shape=(shape,) * 4,
        in_specs=[pl.BlockSpec(memory_space=pltpu.VMEM)] * 4,
        out_specs=(pl.BlockSpec(memory_space=pltpu.HBM),) * 4,
        scratch_shapes=[pltpu.VMEM((4,) + flat_w.shape, F32), pltpu.SemaphoreType.DMA((4, parts))],
        compiler_params=pltpu.CompilerParams(vmem_limit_bytes=16 * 1024 * 1024),
        name="adam",
    )(moved, flat_w, flat_m, flat_v)


def local(NP, NS, pool, batch_index, kernel_scale, cotangent, weights, first_moment, second_moment):
    rows, pair, hidden_units = weights.shape[1:]

    def flatten(a):
        return a.reshape(rows, pair, hidden_units // LANES, LANES).transpose(0, 2, 1, 3).reshape(-1, LANES)

    def unflatten(a):
        a = a.reshape(rows, hidden_units // LANES, pair, LANES).transpose(0, 2, 1, 3)
        return a.reshape(1, rows, pair, hidden_units)

    flat_w = flatten(weights[0])
    moved = stein_transport(NP, NS, kernel_scale, batch_index, flat_w, pool, cotangent[0])
    outs = adam(moved, flat_w, flatten(first_moment[0]), flatten(second_moment[0]))
    return tuple(unflatten(a) for a in outs)


def solution(mesh):
    placed = (
        P("shard", None),
        P("shard"),
        P(),
        P("particle", "shard", None),
        P("particle", "shard", None, None),
        P("particle", "shard", None, None),
        P("particle", "shard", None, None),
    )
    return jax.shard_map(
        functools.partial(local, mesh.shape["particle"], mesh.shape["shard"]),
        mesh=mesh,
        in_specs=placed,
        out_specs=(P("particle", "shard", None, None),) * 4,
        check_vma=False,
    )
```

```python
import functools

import jax
import jax.numpy as jnp
from jax import lax
from jax.experimental import pallas as pl
from jax.experimental.pallas import tpu as pltpu
from jax.sharding import PartitionSpec as P

MESH = pl.DeviceIdType.MESH
CHUNKS = 2
LANES = 128
HIGHEST = lax.Precision.HIGHEST
F32 = jnp.float32
BF16 = jnp.bfloat16


def gelu_pair(up_proj):
    cdf_part = 0.5 * (1.0 + lax.erf(up_proj * 0.7071067811865476))
    density = jnp.exp(-0.5 * up_proj * up_proj) * 0.3989422804014327
    return (up_proj * cdf_part, cdf_part + up_proj * density)


def remote(src, dst, send_sem, recv_sem, device):
    return pltpu.make_async_remote_copy(
        src_ref=src,
        dst_ref=dst,
        send_sem=send_sem,
        recv_sem=recv_sem,
        device_id=device,
        device_id_type=MESH,
    )


def stein_kernel(
    dims,
    scale_hbm, idx_hbm, w_hbm, pool_hbm, cot_hbm,
    out_ref,
    scale_ref, idx_ref, wf, poolv, wbr, wba, wg, na, ca, nt, ct, act, upg, rss, rsr, sc, sa, wa, fld, tr, ta,
    d1, dmine, dpart, dpair, krep,
    load_sem, ex_s, ex_r, cot_s, cot_r, cot_fs, cot_fr, nseg_s, nseg_r, nb_s, nb_r,
    wa_s, wa_r, ag_s, ag_r, rs_s, rs_r, dp_s, dp_r, dh_s, dh_r, sa_s, sa_r, ta_s, ta_r,
):
    NP, NS, RB, TOK, D, FF, POOL = dims
    NZ = NS // 2
    NXY, NX = NP // 2, NP // 4
    G = NX * 2
    NT = FF // LANES
    TC = NT // 2 // CHUNKS
    CH = TC * LANES
    SEG = TOK // G
    HT = TOK // 2
    rem = lax.rem
    p, s = lax.axis_index("particle"), lax.axis_index("shard")
    c, xy = rem(p, 2), p // 2
    x, yl = xy // 2, rem(xy, 2)
    h, z = rem(s, 2), s // 2
    zdev = (
        (p, rem(z + 1, NZ) * 2 + h),
        (p, rem(z + NZ - 1, NZ) * 2 + h),
    )
    sibling = (xy * 2 + 1 - c, s)
    across = (p, z * 2 + 1 - h)
    diagonal = (xy * 2 + 1 - c, z * 2 + 1 - h)
    role = xy * 2 + h

    load_w = pltpu.make_async_copy(w_hbm, wf, load_sem.at[0])
    load_w.start()
    load_pool = pltpu.make_async_copy(pool_hbm, poolv, load_sem.at[1])
    load_pool.start()
    load_idx = pltpu.make_async_copy(idx_hbm, idx_ref, load_sem.at[3])
    load_idx.start()
    load_scale = pltpu.make_async_copy(scale_hbm, scale_ref, load_sem.at[4])
    load_scale.start()
    barrier = pltpu.get_barrier_semaphore()

    def greet(device):
        pl.semaphore_signal(barrier, inc=1, device_id=device, device_id_type=MESH)

    greet(zdev[0])
    greet(zdev[1])
    greet(diagonal)
    for bit in range(1, NZ.bit_length() - 1):
        greet((p, s + (2 << bit) - (4 << bit) * rem(z // (1 << bit), 2)))

    @pl.loop(1, NP)
    def _(d):
        greet((rem(p + d, NP), s))

    @pl.loop(0, NXY)
    def _(o):
        greet((o * 2 + c, z * 2 + 1 - h))

    load_w.wait()
    for half in range(2):
        for k in range(CHUNKS):
            for tile in range(TC):
                for j in range(2):
                    t = (half * CHUNKS + k) * TC + tile
                    v = wf[pl.ds(2 * t + j, RB, stride=2 * NT), :].astype(BF16)
                    wbr[half, k, j, :, tile * LANES:(tile + 1) * LANES] = v
    pl.semaphore_wait(barrier, NP + NXY + NZ.bit_length())

    own_rows = pl.ds(pl.multiple_of((z * 2 + h) * RB, RB), RB)
    sub_at_dest = rem(h + c, 2)

    def exchange(k, half, device):
        return remote(
            wbr.at[half, k], wg.at[k, :, own_rows, :],
            ex_s.at[k * 2 + half], ex_r.at[k * 2 + sub_at_dest], device,
        )

    def cot_half(half):
        part = cot_hbm.at[pl.ds(half * HT, HT)]
        return remote(part, ca.at[h, pl.ds(half * HT, HT)], cot_s.at[half], cot_r.at[1],
                      (xy * 2 + half, z * 2 + 1 - h))

    cot_load = pltpu.make_async_copy(cot_hbm, ca.at[h], load_sem.at[2])
    cot_full = remote(cot_hbm, ca.at[h], cot_s.at[0], cot_r.at[0], sibling)

    @pl.when(c == h)
    def _():
        for k in range(CHUNKS):
            exchange(k, 1 - c, sibling).start()
        for k in range(CHUNKS):
            wg[k, :, own_rows, :] = wbr[c, k]
        cot_load.start()
        cot_full.start()

    @pl.when(c != h)
    def _():
        for k in range(CHUNKS):
            for half in range(2):
                exchange(k, half, (xy * 2 + half, z * 2 + 1 - h)).start()
        for half in range(2):
            cot_half(half).start()

    def exchange_wait(k, sub):
        rows = pl.ds(pl.multiple_of((z * 2 + rem(h + sub, 2)) * RB, RB), RB)
        remote(wbr.at[0, k], wg.at[k, :, rows, :], ex_s.at[0], ex_r.at[k * 2 + sub], sibling).wait_recv()

    FAR = NZ // 2

    def hops(j, way):
        return FAR if j == way else NZ - 1 - FAR

    def slot(k, j, way, step, sub):
        return (((k * 2 + j) * 2 + way) * FAR + step) * 2 + sub

    def ag_copy(k, j, way, step, sub, back):
        b = rem(z + 2 * NZ - step - back, NZ) if way == 0 else rem(z + step + back, NZ)
        rows = pl.ds(pl.multiple_of((b * 2 + rem(h + sub, 2)) * RB, RB), RB)
        n = slot(k, j, way, step, sub)
        return remote(wg.at[k, j, rows, :], wg.at[k, j, rows, :], ag_s.at[n], ag_r.at[n], zdev[way])

    def ag(k, j, way, step, sub):
        return ag_copy(k, j, way, step, sub, 0)

    def ag_first(k, sub):
        for way in range(2):
            for j in range(2):
                ag(k, j, way, 0, sub).start()

    def ag_relay(k, step):
        for sub in range(2):
            for way in range(2):
                for j in range(2):
                    @pl.when(step < hops(j, way))
                    def _():
                        ag_copy(k, j, way, step, sub, 1).wait_recv()

                    @pl.when(step < hops(j, way) - 1)
                    def _():
                        ag(k, j, way, step + 1, sub).start()

    for k in range(CHUNKS):
        @pl.when(c != h)
        def _():
            exchange_wait(k, 0)
        ag_first(k, 0)

    load_pool.wait()
    load_idx.wait()
    load_scale.wait()
    TB = min(LANES, TOK)

    @pl.loop(0, TOK // TB)
    def _(blk):
        at = pl.multiple_of(blk * TB, TB)
        col = jnp.broadcast_to(idx_ref[:, pl.ds(at, TB)], (LANES, TB)).T
        lane = lax.broadcasted_iota(jnp.int32, (TB, LANES), 1)
        onehot = jnp.concatenate(
            [jnp.where(col == lane + i * LANES, 1.0, 0.0).astype(BF16) for i in range(POOL // LANES)], axis=1
        )
        picked = jnp.dot(onehot, poolv[...], preferred_element_type=F32)
        mean = jnp.mean(picked * picked, axis=1, keepdims=True)
        na[h, pl.ds(at, TB), :] = (picked * lax.rsqrt(mean + 1e-06)).astype(BF16)

    seg = x * 2 + c
    own_seg = na.at[h, pl.ds(pl.multiple_of(seg * SEG, SEG), SEG)]
    nseg = remote(own_seg, own_seg, nseg_s, nseg_r, across)
    nseg.start()

    for k in range(CHUNKS):
        exchange_wait(k, 1)
        ag_first(k, 1)

    def slice_out(d):
        q = rem(p + d, NP)
        return remote(wba.at[q], wa.at[p], wa_s.at[d], wa_r.at[d], (q, s))

    def slice_wait(d):
        q = rem(p + NP - d, NP)
        remote(wba.at[q], wa.at[q], wa_s.at[d], wa_r.at[d], (q, s)).wait_recv()

    def send_slices():
        for half in range(2):
            for k in range(CHUNKS):
                for tile in range(TC):
                    for j in range(2):
                        wba[(tile * 2 + j) * 2 + half, k * RB:(k + 1) * RB, :] = (
                            wbr[half, k, j, :, tile * LANES:(tile + 1) * LANES]
                        )

        @pl.loop(1, NP)
        def _(d):
            slice_out(d).start()

        wa[p] = wba[p]

    got_seg = na.at[1 - h, pl.ds(pl.multiple_of(seg * SEG, SEG), SEG)]

    def seg_out(d):
        g = rem(seg + d, G)
        return remote(got_seg, got_seg, nb_s.at[d], nb_r.at[d], ((g // 2 * 2 + yl) * 2 + rem(g, 2), s))

    def seg_wait(d):
        g = rem(seg + G - d, G)
        part = na.at[1 - h, pl.ds(pl.multiple_of(g * SEG, SEG), SEG)]
        remote(part, part, nb_s.at[d], nb_r.at[d], sibling).wait_recv()

    def share_segments():
        remote(got_seg, got_seg, nseg_s, nseg_r, across).wait_recv()

        @pl.loop(1, G)
        def _(d):
            seg_out(d).start()

    cot_mine = ca.at[1 - h, pl.ds(pl.multiple_of(c * HT, HT), HT)]
    cot_other = ca.at[1 - h, pl.ds(pl.multiple_of((1 - c) * HT, HT), HT)]
    cot_pass = remote(cot_mine, cot_mine, cot_fs, cot_fr, sibling)

    def pass_cotangent():
        remote(cot_mine, cot_mine, cot_s.at[0], cot_r.at[1], sibling).wait_recv()
        cot_pass.start()

    eye = lax.broadcasted_iota(jnp.int32, (NP, LANES), 0) == lax.broadcasted_iota(jnp.int32, (NP, LANES), 1)

    def part_out(d):
        q = rem(p + d, NP)
        return remote(dmine, dpart.at[p], dp_s.at[d], dp_r.at[d], (q, s))

    def part_wait(d):
        q = rem(p + NP - d, NP)
        remote(dmine, dpart.at[q], dp_s.at[d], dp_r.at[d], (q, s)).wait_recv()

    def partial_distances():
        @pl.loop(1, NP)
        def _(d):
            slice_wait(d)

        d1[...] = jnp.zeros_like(d1)

        @pl.loop(0, NP)
        def _(i):
            own = wa[i].astype(F32)
            for ahead in range(1, NP // 2 + 1):
                j = rem(i + ahead, NP)
                off = own - wa[j].astype(F32)
                squares = jnp.sum(off * off, axis=0, keepdims=True)
                d1[i, pl.ds(j, 1), :] = squares
                d1[j, pl.ds(i, 1), :] = squares

    def send_distances():
        flat = d1[...].reshape(NP * NP, LANES)
        spread = jnp.dot(flat, jnp.ones((LANES, LANES), F32), precision=HIGHEST, preferred_element_type=F32)
        for i in range(NP):
            dmine[i:i + 1, :] = jnp.sum(
                jnp.where(eye, spread[i * NP:(i + 1) * NP, :], 0.0), axis=0, keepdims=True
            )

        @pl.loop(1, NP)
        def _(d):
            part_out(d).start()

    BITS = NS.bit_length() - 1

    def pair_out(bit):
        mask = 1 << bit
        low = rem(s // mask, 2)
        return remote(dpair.at[bit, 0], dpair.at[bit, 1], dh_s.at[bit], dh_r.at[bit], (p, s + mask - 2 * mask * low))

    def sum_distances(bit):
        if bit == 0:
            dpart[p] = dmine[...]

            @pl.loop(1, NP)
            def _(d):
                part_wait(d)

            total = jnp.sum(dpart[...], axis=0)
        else:
            pair_out(bit - 1).wait_recv()
            total = dpair[bit - 1, 0] + dpair[bit - 1, 1]
        dpair[bit, 0] = total
        if bit < BITS:
            pair_out(bit).start()

    inverse_band = 1.0 / jnp.full((1, LANES), scale_ref[0], jnp.int32).astype(F32)
    repulse = 2.0 * inverse_band

    def kernel_matrix():
        near = jnp.exp(-dpair[BITS, 0] * inverse_band)
        for i in range(NP):
            d1[i] = jnp.where(eye, jnp.broadcast_to(near[i:i + 1, :], (NP, LANES)), 0.0)
        flat = d1[...].reshape(NP * NP, LANES)
        spread = jnp.dot(flat, jnp.ones((LANES, LANES), F32), precision=HIGHEST, preferred_element_type=F32)
        krep[...] = spread.reshape(NP, NP, LANES)

    def turn(source, target, hb, at):
        target[:, pl.ds(pl.multiple_of(hb * TOK + at, HT), HT)] = source[hb, pl.ds(at, HT), :].T

    def hidden(k, blk, flip):
        hb = rem(h + blk // 2, 2)
        at = pl.multiple_of(rem(blk, 2) * HT, HT)
        normed = na[hb, pl.ds(at, HT), :]
        upstream = ca[hb, pl.ds(at, HT), :]
        rows = pl.multiple_of(hb * TOK + at, HT)
        up_proj = jnp.dot(normed, wg[k, 0], preferred_element_type=F32) * D ** (-0.5)
        back_proj = jnp.dot(upstream, wg[k, 1], preferred_element_type=F32) * FF ** (-0.5)
        act_full, gelu_slope = gelu_pair(up_proj)
        act[k, pl.ds(rows, HT), :] = act_full.astype(BF16)
        upg[k, pl.ds(rows, HT), :] = (back_proj * gelu_slope).astype(BF16)
        if flip:
            @pl.when(blk >= 2)
            def _():
                turn(na, nt, hb, at)
                turn(ca, ct, hb, at)

    def gradient(k, j, b):
        lhs = (nt if j == 0 else ct)[pl.ds(pl.multiple_of(b * 2 * RB, 2 * RB), 2 * RB), :]
        return jnp.dot(lhs, (upg if j == 0 else act)[k], preferred_element_type=F32)

    def rs(k, j, way, step, sub):
        n = slot(k, j, way, step, sub)
        return remote(rss.at[n], rsr.at[n], rs_s.at[n], rs_r.at[n], zdev[way])

    def rs_part(k, j, way, step, first):
        left = hops(j, way) - step
        part = gradient(k, j, rem(z + left, NZ) if way == 0 else rem(z + NZ - left, NZ))
        for sub in range(2):
            total = part[sub * RB:(sub + 1) * RB, :]
            n = slot(k, j, way, step, sub)
            if not first:
                rs(k, j, way, step - 1, sub).wait_recv()
                total = total + rsr[n - 2].astype(F32)
            rss[n] = total.astype(BF16)
            rs(k, j, way, step, sub).start()

    def rs_step(k, step, first=False):
        for way in range(2):
            for j in range(2):
                @pl.when(step < hops(j, way))
                def _():
                    rs_part(k, j, way, step, first)

    grad_scale = 1.0 / (TOK * NZ * 2 * D)

    def score_out(k, o, sub):
        return remote(sc.at[k, sub, o], sa.at[k, role], sa_s.at[k * NP + o * 2 + sub], sa_r.at[k * NP + role],
                      (o * 2 + c, z * 2 + sub))

    def rs_final(k):
        parts = [gradient(k, j, z) for j in range(2)]
        for sub in range(2):
            for j in range(2):
                total = parts[j][sub * RB:(sub + 1) * RB, :]
                for way in range(2):
                    rs(k, j, way, hops(j, way) - 1, sub).wait_recv()
                    total = total + rsr[slot(k, j, way, hops(j, way) - 1, sub)].astype(F32)
                factor = (D if j == 0 else FF) ** (-0.5) * grad_scale
                score = (total * -factor).astype(BF16)
                for tile in range(TC):
                    sc[k, sub, tile * 2 + j] = score[:, tile * LANES:(tile + 1) * LANES]
                for n in range(TC):
                    o = rem(xy // 2 + n, TC) * 2 + j

                    @pl.when(o * 2 + sub != role)
                    def _():
                        score_out(k, o, sub).start()

        sa[k, role] = sc[k, h, xy]

    def transport_out(k, d):
        q = rem(p + d, NP)
        return remote(tr.at[k, q], ta.at[k, p], ta_s.at[k * NP + d], ta_r.at[k * NP + d], (q, s))

    def transport_wait(k, d):
        q = rem(p + NP - d, NP)
        remote(tr.at[k, 0], ta.at[k, q], ta_s.at[k * NP + d], ta_r.at[k * NP + d], sibling).wait_recv()

    params_total = 2 * D * FF

    def move(k):
        for q in range(NP):
            @pl.when(q != role)
            def _():
                remote(sc.at[k, 0, 0], sa.at[k, q], sa_s.at[0], sa_r.at[k * NP + q], sibling).wait_recv()

            fld[q] = sa[k, q].astype(F32) - repulse * wa[q, k * RB:(k + 1) * RB, :].astype(F32)

        @pl.loop(1, NP + 1)
        def _(d):
            i = rem(p + d, NP)
            weighted = krep[i, 0:1, :] * fld[0]
            for j in range(1, NP):
                weighted = weighted + krep[i, j:j + 1, :] * fld[j]
            kernel_total = jnp.sum(krep[i], axis=0, keepdims=True)
            own_w = wa[i, k * RB:(k + 1) * RB, :].astype(F32)
            tr[k, i] = (params_total / NP * (weighted + repulse * kernel_total * own_w)).astype(BF16)

            @pl.when(d < NP)
            def _():
                transport_out(k, d).start()

        ta[k, p] = tr[k, p]

    def collect(k):
        @pl.loop(1, NP)
        def _(d):
            transport_wait(k, d)

        out_ref[k] = ta[k]

    def drain_gather():
        @pl.when(c == h)
        def _():
            for k in range(CHUNKS):
                exchange(k, 1 - c, sibling).wait_send()
            cot_full.wait_send()

        @pl.when(c != h)
        def _():
            for k in range(CHUNKS):
                for half in range(2):
                    exchange(k, half, (xy * 2 + half, z * 2 + 1 - h)).wait_send()
            for half in range(2):
                cot_half(half).wait_send()

        nseg.wait_send()
        cot_pass.wait_send()

        @pl.loop(1, G)
        def _(d):
            seg_out(d).wait_send()

        @pl.loop(1, NP)
        def _(d):
            slice_out(d).wait_send()
            part_out(d).wait_send()

        for k in range(CHUNKS):
            for j in range(2):
                for way in range(2):
                    @pl.loop(0, hops(j, way))
                    def _(step):
                        for sub in range(2):
                            ag(k, j, way, step, sub).wait_send()

    def drain_ring():
        for bit in range(BITS):
            pair_out(bit).wait_send()

        for k in range(CHUNKS):
            for j in range(2):
                for way in range(2):
                    @pl.loop(0, hops(j, way))
                    def _(step):
                        for sub in range(2):
                            rs(k, j, way, step, sub).wait_send()

    def drain_scores():
        for k in range(CHUNKS):
            for o in range(NXY):
                for sub in range(2):
                    @pl.when(o * 2 + sub != role)
                    def _():
                        score_out(k, o, sub).wait_send()

    def drain_transport():
        @pl.loop(1, NP)
        def _(d):
            for k in range(CHUNKS):
                transport_out(k, d).wait_send()

    ag_relay(0, 0)
    for half in range(2):
        turn(na, nt, h, half * HT)
    ag_relay(0, 1)
    share_segments()

    @pl.when(c == h)
    def _():
        cot_load.wait()

    @pl.when(c != h)
    def _():
        remote(cot_hbm, ca.at[h], cot_s.at[0], cot_r.at[0], sibling).wait_recv()

    for half in range(2):
        turn(ca, ct, h, half * HT)
    ag_relay(0, 2)
    ag_relay(1, 0)
    ag_relay(0, 3)
    pass_cotangent()
    send_slices()

    @pl.loop(0, 4)
    def _(blk):
        @pl.when(blk == 2)
        def _():
            @pl.loop(1, G)
            def _(d):
                seg_wait(d)

            remote(cot_other, cot_other, cot_fs, cot_fr, sibling).wait_recv()

        hidden(0, blk, True)

        @pl.when(blk < 2)
        def _():
            ag_relay(1, blk + 1)

    rs_step(0, 0, True)
    ag_relay(1, 3)

    @pl.loop(0, 4)
    def _(blk):
        hidden(1, blk, False)

        @pl.when(blk < 3)
        def _():
            rs_step(0, blk + 1)

        @pl.when(blk == 0)
        def _():
            partial_distances()
            send_distances()

        for bit in range(2):
            @pl.when(blk == bit + 2)
            def _():
                sum_distances(bit)

    rs_step(1, 0, True)
    rs_final(0)
    sum_distances(2)
    drain_gather()
    rs_step(1, 1)
    for bit in range(3, BITS):
        sum_distances(bit)
    rs_step(1, 2)
    sum_distances(BITS)
    kernel_matrix()
    rs_step(1, 3)
    move(0)
    rs_final(1)
    collect(0)
    drain_ring()
    move(1)
    drain_scores()
    collect(1)
    drain_transport()


def stein_transport(NP, NS, kernel_scale, batch_index, flat_w, pool, cotangent):
    NZ = NS // 2
    TOK, D = cotangent.shape
    RB = D // NS
    FF = flat_w.shape[0] * LANES // RB // 2
    POOL = pool.shape[0]
    NXY, G = NP // 2, NP // 2
    TC = FF // LANES // 2 // CHUNKS
    CH = TC * LANES
    assert TC * 2 == NXY
    dma = pltpu.SemaphoreType.DMA
    ring = CHUNKS * 2 * 2 * (NZ // 2) * 2
    scratch = [
        pltpu.SMEM((1,), jnp.int32),
        pltpu.VMEM((1, TOK), jnp.int32),
        pltpu.VMEM(flat_w.shape, F32),
        pltpu.VMEM((POOL, D), BF16),
        pltpu.VMEM((2, CHUNKS, 2, RB, CH), BF16),
        pltpu.VMEM((NP, CHUNKS * RB, LANES), BF16),
        pltpu.VMEM((CHUNKS, 2, D, CH), BF16),
        pltpu.VMEM((2, TOK, D), BF16),
        pltpu.VMEM((2, TOK, D), BF16),
        pltpu.VMEM((D, 2 * TOK), BF16),
        pltpu.VMEM((D, 2 * TOK), BF16),
        pltpu.VMEM((CHUNKS, 2 * TOK, CH), BF16),
        pltpu.VMEM((CHUNKS, 2 * TOK, CH), BF16),
        pltpu.VMEM((ring, RB, CH), BF16),
        pltpu.VMEM((ring, RB, CH), BF16),
        pltpu.VMEM((CHUNKS, 2, NXY, RB, LANES), BF16),
        pltpu.VMEM((CHUNKS, NP, RB, LANES), BF16),
        pltpu.VMEM((NP, CHUNKS * RB, LANES), BF16),
        pltpu.VMEM((NP, RB, LANES), F32),
        pltpu.VMEM((CHUNKS, NP, RB, LANES), BF16),
        pltpu.VMEM((CHUNKS, NP, RB, LANES), BF16),
        pltpu.VMEM((NP, NP, LANES), F32),
        pltpu.VMEM((NP, LANES), F32),
        pltpu.VMEM((NP, NP, LANES), F32),
        pltpu.VMEM((NS.bit_length(), 2, NP, LANES), F32),
        pltpu.VMEM((NP, NP, LANES), F32),
        dma((5,)),
        dma((2 * CHUNKS,)), dma((2 * CHUNKS,)),
        dma((2,)), dma((2,)), dma(()), dma(()),
        dma(()), dma(()), dma((G,)), dma((G,)),
        dma((NP,)), dma((NP,)),
        dma((ring,)), dma((ring,)), dma((ring,)), dma((ring,)),
        dma((NP,)), dma((NP,)), dma((NS.bit_length(),)), dma((NS.bit_length(),)),
        dma((CHUNKS * NP,)), dma((CHUNKS * NP,)), dma((CHUNKS * NP,)), dma((CHUNKS * NP,)),
    ]
    anywhere = pl.BlockSpec(memory_space=pltpu.HBM)
    vmem = pl.BlockSpec(memory_space=pltpu.VMEM)
    return pl.pallas_call(
        functools.partial(stein_kernel, (NP, NS, RB, TOK, D, FF, POOL)),
        out_shape=jax.ShapeDtypeStruct((CHUNKS, NP, RB, LANES), BF16),
        in_specs=[anywhere] * 5,
        out_specs=vmem,
        scratch_shapes=scratch,
        compiler_params=pltpu.CompilerParams(
            collective_id=0, has_side_effects=True, vmem_limit_bytes=56 * 1024 * 1024
        ),
        name="stein",
    )(kernel_scale, batch_index.reshape(1, TOK), flat_w, pool, cotangent)


def adam_kernel(NT, parts, moved_ref, w_ref, m_ref, v_ref, new_w, new_m, new_v, transport_ref, out, sems):
    NP, rows = moved_ref.shape[1:3]
    TC = NT // 2 // CHUNKS
    part_rows = rows // parts
    size = part_rows * 2 * NT
    copies = []
    for part in range(parts):
        span = pl.ds(part * size, size)
        for k in range(CHUNKS):
            for q in range(NP):
                o, half = q // 2, q % 2
                t = (half * CHUNKS + k) * TC + o // 2
                piece = moved_ref[k, q, part * part_rows:(part + 1) * part_rows, :].astype(F32)
                out[0, pl.ds(part * size + 2 * t + o % 2, part_rows, stride=2 * NT), :] = piece
        transport = out[0, span, :]
        new_first = 0.9 * m_ref[span, :] - 0.1 * transport
        new_second = 0.999 * v_ref[span, :] + 0.001 * transport * transport
        out[1, span, :] = new_first
        out[2, span, :] = new_second
        out[3, span, :] = w_ref[span, :] - 0.01 * new_first / (jnp.sqrt(new_second) + 1e-08)
        for n, target in enumerate((transport_ref, new_m, new_v, new_w)):
            copy = pltpu.make_async_copy(out.at[n, span], target.at[span], sems.at[n, part])
            copy.start()
            copies.append(copy)
    for copy in copies:
        copy.wait()


def adam(moved, flat_w, flat_m, flat_v):
    RB, lanes = moved.shape[2:]
    parts = max(RB // 16, 1)
    shape = jax.ShapeDtypeStruct(flat_w.shape, F32)
    return pl.pallas_call(
        functools.partial(adam_kernel, flat_w.shape[0] // RB // 2, parts),
        out_shape=(shape,) * 4,
        in_specs=[pl.BlockSpec(memory_space=pltpu.VMEM)] * 4,
        out_specs=(pl.BlockSpec(memory_space=pltpu.HBM),) * 4,
        scratch_shapes=[pltpu.VMEM((4,) + flat_w.shape, F32), pltpu.SemaphoreType.DMA((4, parts))],
        compiler_params=pltpu.CompilerParams(vmem_limit_bytes=16 * 1024 * 1024),
        name="adam",
    )(moved, flat_w, flat_m, flat_v)


def local(NP, NS, pool, batch_index, kernel_scale, cotangent, weights, first_moment, second_moment):
    rows, pair, hidden_units = weights.shape[1:]

    def flatten(a):
        return a.reshape(rows, pair, hidden_units // LANES, LANES).transpose(0, 2, 1, 3).reshape(-1, LANES)

    def unflatten(a):
        a = a.reshape(rows, hidden_units // LANES, pair, LANES).transpose(0, 2, 1, 3)
        return a.reshape(1, rows, pair, hidden_units)

    flat_w = flatten(weights[0])
    moved = stein_transport(NP, NS, kernel_scale, batch_index, flat_w, pool, cotangent[0])
    outs = adam(moved, flat_w, flatten(first_moment[0]), flatten(second_moment[0]))
    return tuple(unflatten(a) for a in outs)


def solution(mesh):
    placed = (
        P("shard", None),
        P("shard"),
        P(),
        P("particle", "shard", None),
        P("particle", "shard", None, None),
        P("particle", "shard", None, None),
        P("particle", "shard", None, None),
    )
    return jax.shard_map(
        functools.partial(local, mesh.shape["particle"], mesh.shape["shard"]),
        mesh=mesh,
        in_specs=placed,
        out_specs=(P("particle", "shard", None, None),) * 4,
        check_vma=False,
    )
```

```python
import functools

import jax
import jax.numpy as jnp
from jax import lax
from jax.experimental import pallas as pl
from jax.experimental.pallas import tpu as pltpu
from jax.sharding import PartitionSpec as P

MESH = pl.DeviceIdType.MESH
CHUNKS = 2
LANES = 128
HIGHEST = lax.Precision.HIGHEST
F32 = jnp.float32
BF16 = jnp.bfloat16


def gelu_pair(up_proj):
    cdf_part = 0.5 * (1.0 + lax.erf(up_proj * 0.7071067811865476))
    density = jnp.exp(-0.5 * up_proj * up_proj) * 0.3989422804014327
    return (up_proj * cdf_part, cdf_part + up_proj * density)


def remote(src, dst, send_sem, recv_sem, device):
    return pltpu.make_async_remote_copy(
        src_ref=src,
        dst_ref=dst,
        send_sem=send_sem,
        recv_sem=recv_sem,
        device_id=device,
        device_id_type=MESH,
    )


def stein_kernel(
    dims,
    scale_hbm, idx_hbm, w_hbm, pool_hbm, cot_hbm,
    out_ref,
    scale_ref, idx_ref, wf, poolv, wbr, wba, wg, na, ca, nt, ct, act, upg, rss, rsr, sc, sa, wa, fld, tr, ta,
    d1, dmine, dpart, dpair, krep,
    load_sem, ex_s, ex_r, cot_s, cot_r, cot_fs, cot_fr, nseg_s, nseg_r, nb_s, nb_r,
    wa_s, wa_r, ag_s, ag_r, rs_s, rs_r, dp_s, dp_r, dh_s, dh_r, sa_s, sa_r, ta_s, ta_r,
):
    NP, NS, RB, TOK, D, FF, POOL = dims
    NZ = NS // 2
    NXY, NX = NP // 2, NP // 4
    G = NX * 2
    NT = FF // LANES
    TC = NT // 2 // CHUNKS
    CH = TC * LANES
    SEG = TOK // G
    HT = TOK // 2
    rem = lax.rem
    p, s = lax.axis_index("particle"), lax.axis_index("shard")
    c, xy = rem(p, 2), p // 2
    x, yl = xy // 2, rem(xy, 2)
    h, z = rem(s, 2), s // 2
    zdev = (
        (p, rem(z + 1, NZ) * 2 + h),
        (p, rem(z + NZ - 1, NZ) * 2 + h),
    )
    sibling = (xy * 2 + 1 - c, s)
    across = (p, z * 2 + 1 - h)
    diagonal = (xy * 2 + 1 - c, z * 2 + 1 - h)
    role = xy * 2 + h

    load_w = pltpu.make_async_copy(w_hbm, wf, load_sem.at[0])
    load_w.start()
    load_pool = pltpu.make_async_copy(pool_hbm, poolv, load_sem.at[1])
    load_pool.start()
    load_idx = pltpu.make_async_copy(idx_hbm, idx_ref, load_sem.at[3])
    load_idx.start()
    load_scale = pltpu.make_async_copy(scale_hbm, scale_ref, load_sem.at[4])
    load_scale.start()
    barrier = pltpu.get_barrier_semaphore()

    def greet(device):
        pl.semaphore_signal(barrier, inc=1, device_id=device, device_id_type=MESH)

    greet(zdev[0])
    greet(zdev[1])
    greet(diagonal)
    for bit in range(1, NZ.bit_length() - 1):
        greet((p, s + (2 << bit) - (4 << bit) * rem(z // (1 << bit), 2)))

    @pl.loop(1, NP)
    def _(d):
        greet((rem(p + d, NP), s))

    @pl.loop(0, NXY)
    def _(o):
        greet((o * 2 + c, z * 2 + 1 - h))

    load_w.wait()
    def round_weights(k):
        for half in range(2):
            for tile in range(TC):
                for j in range(2):
                    t = (half * CHUNKS + k) * TC + tile
                    v = wf[pl.ds(2 * t + j, RB, stride=2 * NT), :].astype(BF16)
                    wbr[half, k, j, :, tile * LANES:(tile + 1) * LANES] = v

    round_weights(0)
    pl.semaphore_wait(barrier, NP + NXY + NZ.bit_length())

    own_rows = pl.ds(pl.multiple_of((z * 2 + h) * RB, RB), RB)
    sub_at_dest = rem(h + c, 2)

    def exchange(k, half, device):
        return remote(
            wbr.at[half, k], wg.at[k, :, own_rows, :],
            ex_s.at[k * 2 + half], ex_r.at[k * 2 + sub_at_dest], device,
        )

    def cot_half(half):
        part = cot_hbm.at[pl.ds(half * HT, HT)]
        return remote(part, ca.at[h, pl.ds(half * HT, HT)], cot_s.at[half], cot_r.at[1],
                      (xy * 2 + half, z * 2 + 1 - h))

    cot_load = pltpu.make_async_copy(cot_hbm, ca.at[h], load_sem.at[2])
    cot_full = remote(cot_hbm, ca.at[h], cot_s.at[0], cot_r.at[0], sibling)

    for k in range(CHUNKS):
        if k > 0:
            round_weights(k)

        @pl.when(c == h)
        def _():
            exchange(k, 1 - c, sibling).start()
            wg[k, :, own_rows, :] = wbr[c, k]

        @pl.when(c != h)
        def _():
            for half in range(2):
                exchange(k, half, (xy * 2 + half, z * 2 + 1 - h)).start()

    @pl.when(c == h)
    def _():
        cot_load.start()
        cot_full.start()

    @pl.when(c != h)
    def _():
        for half in range(2):
            cot_half(half).start()

    def exchange_wait(k, sub):
        rows = pl.ds(pl.multiple_of((z * 2 + rem(h + sub, 2)) * RB, RB), RB)
        remote(wbr.at[0, k], wg.at[k, :, rows, :], ex_s.at[0], ex_r.at[k * 2 + sub], sibling).wait_recv()

    FAR = NZ // 2

    def hops(j, way):
        return FAR if j == way else NZ - 1 - FAR

    def slot(k, j, way, step, sub):
        return (((k * 2 + j) * 2 + way) * FAR + step) * 2 + sub

    def ag_copy(k, j, way, step, sub, back):
        b = rem(z + 2 * NZ - step - back, NZ) if way == 0 else rem(z + step + back, NZ)
        rows = pl.ds(pl.multiple_of((b * 2 + rem(h + sub, 2)) * RB, RB), RB)
        n = slot(k, j, way, step, sub)
        return remote(wg.at[k, j, rows, :], wg.at[k, j, rows, :], ag_s.at[n], ag_r.at[n], zdev[way])

    def ag(k, j, way, step, sub):
        return ag_copy(k, j, way, step, sub, 0)

    def ag_first(k, sub):
        for way in range(2):
            for j in range(2):
                ag(k, j, way, 0, sub).start()

    def ag_relay(k, step):
        for sub in range(2):
            for way in range(2):
                for j in range(2):
                    @pl.when(step < hops(j, way))
                    def _():
                        ag_copy(k, j, way, step, sub, 1).wait_recv()

                    @pl.when(step < hops(j, way) - 1)
                    def _():
                        ag(k, j, way, step + 1, sub).start()

    for k in range(CHUNKS):
        @pl.when(c != h)
        def _():
            exchange_wait(k, 0)
        ag_first(k, 0)

    load_pool.wait()
    load_idx.wait()
    load_scale.wait()
    TB = min(LANES, TOK)

    @pl.loop(0, TOK // TB)
    def _(blk):
        at = pl.multiple_of(blk * TB, TB)
        col = jnp.broadcast_to(idx_ref[:, pl.ds(at, TB)], (LANES, TB)).T
        lane = lax.broadcasted_iota(jnp.int32, (TB, LANES), 1)
        onehot = jnp.concatenate(
            [jnp.where(col == lane + i * LANES, 1.0, 0.0).astype(BF16) for i in range(POOL // LANES)], axis=1
        )
        picked = jnp.dot(onehot, poolv[...], preferred_element_type=F32)
        mean = jnp.mean(picked * picked, axis=1, keepdims=True)
        na[h, pl.ds(at, TB), :] = (picked * lax.rsqrt(mean + 1e-06)).astype(BF16)

    seg = x * 2 + c
    own_seg = na.at[h, pl.ds(pl.multiple_of(seg * SEG, SEG), SEG)]
    nseg = remote(own_seg, own_seg, nseg_s, nseg_r, across)
    nseg.start()

    for k in range(CHUNKS):
        exchange_wait(k, 1)
        ag_first(k, 1)

    def slice_out(d):
        q = rem(p + d, NP)
        return remote(wba.at[q], wa.at[p], wa_s.at[d], wa_r.at[d], (q, s))

    def slice_wait(d):
        q = rem(p + NP - d, NP)
        remote(wba.at[q], wa.at[q], wa_s.at[d], wa_r.at[d], (q, s)).wait_recv()

    def send_slices():
        for half in range(2):
            for k in range(CHUNKS):
                for tile in range(TC):
                    for j in range(2):
                        wba[(tile * 2 + j) * 2 + half, k * RB:(k + 1) * RB, :] = (
                            wbr[half, k, j, :, tile * LANES:(tile + 1) * LANES]
                        )

        @pl.loop(1, NP)
        def _(d):
            slice_out(d).start()

        wa[p] = wba[p]

    got_seg = na.at[1 - h, pl.ds(pl.multiple_of(seg * SEG, SEG), SEG)]

    def seg_out(d):
        g = rem(seg + d, G)
        return remote(got_seg, got_seg, nb_s.at[d], nb_r.at[d], ((g // 2 * 2 + yl) * 2 + rem(g, 2), s))

    def seg_wait(d):
        g = rem(seg + G - d, G)
        part = na.at[1 - h, pl.ds(pl.multiple_of(g * SEG, SEG), SEG)]
        remote(part, part, nb_s.at[d], nb_r.at[d], sibling).wait_recv()

    def share_segments():
        remote(got_seg, got_seg, nseg_s, nseg_r, across).wait_recv()

        @pl.loop(1, G)
        def _(d):
            seg_out(d).start()

    cot_mine = ca.at[1 - h, pl.ds(pl.multiple_of(c * HT, HT), HT)]
    cot_other = ca.at[1 - h, pl.ds(pl.multiple_of((1 - c) * HT, HT), HT)]
    cot_pass = remote(cot_mine, cot_mine, cot_fs, cot_fr, sibling)

    def pass_cotangent():
        remote(cot_mine, cot_mine, cot_s.at[0], cot_r.at[1], sibling).wait_recv()
        cot_pass.start()

    eye = lax.broadcasted_iota(jnp.int32, (NP, LANES), 0) == lax.broadcasted_iota(jnp.int32, (NP, LANES), 1)

    def part_out(d):
        q = rem(p + d, NP)
        return remote(dmine, dpart.at[p], dp_s.at[d], dp_r.at[d], (q, s))

    def part_wait(d):
        q = rem(p + NP - d, NP)
        remote(dmine, dpart.at[q], dp_s.at[d], dp_r.at[d], (q, s)).wait_recv()

    def partial_distances():
        @pl.loop(1, NP)
        def _(d):
            slice_wait(d)

        d1[...] = jnp.zeros_like(d1)

        @pl.loop(0, NP)
        def _(i):
            own = wa[i].astype(F32)
            for ahead in range(1, NP // 2 + 1):
                j = rem(i + ahead, NP)
                off = own - wa[j].astype(F32)
                squares = jnp.sum(off * off, axis=0, keepdims=True)
                d1[i, pl.ds(j, 1), :] = squares
                d1[j, pl.ds(i, 1), :] = squares

    def send_distances():
        flat = d1[...].reshape(NP * NP, LANES)
        spread = jnp.dot(flat, jnp.ones((LANES, LANES), F32), precision=HIGHEST, preferred_element_type=F32)
        for i in range(NP):
            dmine[i:i + 1, :] = jnp.sum(
                jnp.where(eye, spread[i * NP:(i + 1) * NP, :], 0.0), axis=0, keepdims=True
            )

        @pl.loop(1, NP)
        def _(d):
            part_out(d).start()

    BITS = NS.bit_length() - 1

    def pair_out(bit):
        mask = 1 << bit
        low = rem(s // mask, 2)
        return remote(dpair.at[bit, 0], dpair.at[bit, 1], dh_s.at[bit], dh_r.at[bit], (p, s + mask - 2 * mask * low))

    def sum_distances(bit):
        if bit == 0:
            dpart[p] = dmine[...]

            @pl.loop(1, NP)
            def _(d):
                part_wait(d)

            total = jnp.sum(dpart[...], axis=0)
        else:
            pair_out(bit - 1).wait_recv()
            total = dpair[bit - 1, 0] + dpair[bit - 1, 1]
        dpair[bit, 0] = total
        if bit < BITS:
            pair_out(bit).start()

    inverse_band = 1.0 / jnp.full((1, LANES), scale_ref[0], jnp.int32).astype(F32)
    repulse = 2.0 * inverse_band

    def kernel_matrix():
        near = jnp.exp(-dpair[BITS, 0] * inverse_band)
        for i in range(NP):
            d1[i] = jnp.where(eye, jnp.broadcast_to(near[i:i + 1, :], (NP, LANES)), 0.0)
        flat = d1[...].reshape(NP * NP, LANES)
        spread = jnp.dot(flat, jnp.ones((LANES, LANES), F32), precision=HIGHEST, preferred_element_type=F32)
        krep[...] = spread.reshape(NP, NP, LANES)

    def turn(source, target, hb, at):
        target[:, pl.ds(pl.multiple_of(hb * TOK + at, HT), HT)] = source[hb, pl.ds(at, HT), :].T

    def hidden(k, blk, flip):
        hb = rem(h + blk // 2, 2)
        at = pl.multiple_of(rem(blk, 2) * HT, HT)
        normed = na[hb, pl.ds(at, HT), :]
        upstream = ca[hb, pl.ds(at, HT), :]
        rows = pl.multiple_of(hb * TOK + at, HT)
        up_proj = jnp.dot(normed, wg[k, 0], preferred_element_type=F32) * D ** (-0.5)
        back_proj = jnp.dot(upstream, wg[k, 1], preferred_element_type=F32) * FF ** (-0.5)
        act_full, gelu_slope = gelu_pair(up_proj)
        act[k, pl.ds(rows, HT), :] = act_full.astype(BF16)
        upg[k, pl.ds(rows, HT), :] = (back_proj * gelu_slope).astype(BF16)
        if flip:
            @pl.when(blk >= 2)
            def _():
                turn(na, nt, hb, at)
                turn(ca, ct, hb, at)

    def gradient(k, j, b):
        lhs = (nt if j == 0 else ct)[pl.ds(pl.multiple_of(b * 2 * RB, 2 * RB), 2 * RB), :]
        return jnp.dot(lhs, (upg if j == 0 else act)[k], preferred_element_type=F32)

    def rs(k, j, way, step, sub):
        n = slot(k, j, way, step, sub)
        return remote(rss.at[n], rsr.at[n], rs_s.at[n], rs_r.at[n], zdev[way])

    def rs_part(k, j, way, step, first):
        left = hops(j, way) - step
        part = gradient(k, j, rem(z + left, NZ) if way == 0 else rem(z + NZ - left, NZ))
        for sub in range(2):
            total = part[sub * RB:(sub + 1) * RB, :]
            n = slot(k, j, way, step, sub)
            if not first:
                rs(k, j, way, step - 1, sub).wait_recv()
                total = total + rsr[n - 2].astype(F32)
            rss[n] = total.astype(BF16)
            rs(k, j, way, step, sub).start()

    def rs_step(k, step, first=False):
        for way in range(2):
            for j in range(2):
                @pl.when(step < hops(j, way))
                def _():
                    rs_part(k, j, way, step, first)

    grad_scale = 1.0 / (TOK * NZ * 2 * D)

    def score_out(k, o, sub):
        return remote(sc.at[k, sub, o], sa.at[k, role], sa_s.at[k * NP + o * 2 + sub], sa_r.at[k * NP + role],
                      (o * 2 + c, z * 2 + sub))

    def rs_final(k):
        parts = [gradient(k, j, z) for j in range(2)]
        for sub in range(2):
            for j in range(2):
                total = parts[j][sub * RB:(sub + 1) * RB, :]
                for way in range(2):
                    rs(k, j, way, hops(j, way) - 1, sub).wait_recv()
                    total = total + rsr[slot(k, j, way, hops(j, way) - 1, sub)].astype(F32)
                factor = (D if j == 0 else FF) ** (-0.5) * grad_scale
                score = (total * -factor).astype(BF16)
                for tile in range(TC):
                    sc[k, sub, tile * 2 + j] = score[:, tile * LANES:(tile + 1) * LANES]
                for n in range(TC):
                    o = rem(xy // 2 + n, TC) * 2 + j

                    @pl.when(o * 2 + sub != role)
                    def _():
                        score_out(k, o, sub).start()

        sa[k, role] = sc[k, h, xy]

    def transport_out(k, d):
        q = rem(p + d, NP)
        return remote(tr.at[k, q], ta.at[k, p], ta_s.at[k * NP + d], ta_r.at[k * NP + d], (q, s))

    def transport_wait(k, d):
        q = rem(p + NP - d, NP)
        remote(tr.at[k, 0], ta.at[k, q], ta_s.at[k * NP + d], ta_r.at[k * NP + d], sibling).wait_recv()

    params_total = 2 * D * FF

    def move(k):
        for q in range(NP):
            @pl.when(q != role)
            def _():
                remote(sc.at[k, 0, 0], sa.at[k, q], sa_s.at[0], sa_r.at[k * NP + q], sibling).wait_recv()

            fld[q] = sa[k, q].astype(F32) - repulse * wa[q, k * RB:(k + 1) * RB, :].astype(F32)

        @pl.loop(1, NP + 1)
        def _(d):
            i = rem(p + d, NP)
            weighted = krep[i, 0:1, :] * fld[0]
            for j in range(1, NP):
                weighted = weighted + krep[i, j:j + 1, :] * fld[j]
            kernel_total = jnp.sum(krep[i], axis=0, keepdims=True)
            own_w = wa[i, k * RB:(k + 1) * RB, :].astype(F32)
            tr[k, i] = (params_total / NP * (weighted + repulse * kernel_total * own_w)).astype(BF16)

            @pl.when(d < NP)
            def _():
                transport_out(k, d).start()

        ta[k, p] = tr[k, p]

    def collect(k):
        @pl.loop(1, NP)
        def _(d):
            transport_wait(k, d)

        out_ref[k] = ta[k]

    def drain_gather():
        @pl.when(c == h)
        def _():
            for k in range(CHUNKS):
                exchange(k, 1 - c, sibling).wait_send()
            cot_full.wait_send()

        @pl.when(c != h)
        def _():
            for k in range(CHUNKS):
                for half in range(2):
                    exchange(k, half, (xy * 2 + half, z * 2 + 1 - h)).wait_send()
            for half in range(2):
                cot_half(half).wait_send()

        nseg.wait_send()
        cot_pass.wait_send()

        @pl.loop(1, G)
        def _(d):
            seg_out(d).wait_send()

        @pl.loop(1, NP)
        def _(d):
            slice_out(d).wait_send()
            part_out(d).wait_send()

        for k in range(CHUNKS):
            for j in range(2):
                for way in range(2):
                    @pl.loop(0, hops(j, way))
                    def _(step):
                        for sub in range(2):
                            ag(k, j, way, step, sub).wait_send()

    def drain_ring():
        for bit in range(BITS):
            pair_out(bit).wait_send()

        for k in range(CHUNKS):
            for j in range(2):
                for way in range(2):
                    @pl.loop(0, hops(j, way))
                    def _(step):
                        for sub in range(2):
                            rs(k, j, way, step, sub).wait_send()

    def drain_scores():
        for k in range(CHUNKS):
            for o in range(NXY):
                for sub in range(2):
                    @pl.when(o * 2 + sub != role)
                    def _():
                        score_out(k, o, sub).wait_send()

    def drain_transport():
        @pl.loop(1, NP)
        def _(d):
            for k in range(CHUNKS):
                transport_out(k, d).wait_send()

    ag_relay(0, 0)
    for half in range(2):
        turn(na, nt, h, half * HT)
    ag_relay(0, 1)
    share_segments()

    @pl.when(c == h)
    def _():
        cot_load.wait()

    @pl.when(c != h)
    def _():
        remote(cot_hbm, ca.at[h], cot_s.at[0], cot_r.at[0], sibling).wait_recv()

    for half in range(2):
        turn(ca, ct, h, half * HT)
    ag_relay(0, 2)
    ag_relay(1, 0)
    ag_relay(0, 3)
    pass_cotangent()
    send_slices()

    @pl.loop(0, 4)
    def _(blk):
        @pl.when(blk == 2)
        def _():
            @pl.loop(1, G)
            def _(d):
                seg_wait(d)

            remote(cot_other, cot_other, cot_fs, cot_fr, sibling).wait_recv()

        hidden(0, blk, True)

        @pl.when(blk < 2)
        def _():
            ag_relay(1, blk + 1)

    rs_step(0, 0, True)
    ag_relay(1, 3)

    @pl.loop(0, 4)
    def _(blk):
        hidden(1, blk, False)

        @pl.when(blk < 3)
        def _():
            rs_step(0, blk + 1)

        @pl.when(blk == 0)
        def _():
            partial_distances()
            send_distances()

        for bit in range(2):
            @pl.when(blk == bit + 2)
            def _():
                sum_distances(bit)

    rs_step(1, 0, True)
    rs_final(0)
    sum_distances(2)
    drain_gather()
    rs_step(1, 1)
    for bit in range(3, BITS):
        sum_distances(bit)
    rs_step(1, 2)
    sum_distances(BITS)
    kernel_matrix()
    rs_step(1, 3)
    move(0)
    rs_final(1)
    collect(0)
    drain_ring()
    move(1)
    drain_scores()
    collect(1)
    drain_transport()


def stein_transport(NP, NS, kernel_scale, batch_index, flat_w, pool, cotangent):
    NZ = NS // 2
    TOK, D = cotangent.shape
    RB = D // NS
    FF = flat_w.shape[0] * LANES // RB // 2
    POOL = pool.shape[0]
    NXY, G = NP // 2, NP // 2
    TC = FF // LANES // 2 // CHUNKS
    CH = TC * LANES
    assert TC * 2 == NXY
    dma = pltpu.SemaphoreType.DMA
    ring = CHUNKS * 2 * 2 * (NZ // 2) * 2
    scratch = [
        pltpu.SMEM((1,), jnp.int32),
        pltpu.VMEM((1, TOK), jnp.int32),
        pltpu.VMEM(flat_w.shape, F32),
        pltpu.VMEM((POOL, D), BF16),
        pltpu.VMEM((2, CHUNKS, 2, RB, CH), BF16),
        pltpu.VMEM((NP, CHUNKS * RB, LANES), BF16),
        pltpu.VMEM((CHUNKS, 2, D, CH), BF16),
        pltpu.VMEM((2, TOK, D), BF16),
        pltpu.VMEM((2, TOK, D), BF16),
        pltpu.VMEM((D, 2 * TOK), BF16),
        pltpu.VMEM((D, 2 * TOK), BF16),
        pltpu.VMEM((CHUNKS, 2 * TOK, CH), BF16),
        pltpu.VMEM((CHUNKS, 2 * TOK, CH), BF16),
        pltpu.VMEM((ring, RB, CH), BF16),
        pltpu.VMEM((ring, RB, CH), BF16),
        pltpu.VMEM((CHUNKS, 2, NXY, RB, LANES), BF16),
        pltpu.VMEM((CHUNKS, NP, RB, LANES), BF16),
        pltpu.VMEM((NP, CHUNKS * RB, LANES), BF16),
        pltpu.VMEM((NP, RB, LANES), F32),
        pltpu.VMEM((CHUNKS, NP, RB, LANES), BF16),
        pltpu.VMEM((CHUNKS, NP, RB, LANES), BF16),
        pltpu.VMEM((NP, NP, LANES), F32),
        pltpu.VMEM((NP, LANES), F32),
        pltpu.VMEM((NP, NP, LANES), F32),
        pltpu.VMEM((NS.bit_length(), 2, NP, LANES), F32),
        pltpu.VMEM((NP, NP, LANES), F32),
        dma((5,)),
        dma((2 * CHUNKS,)), dma((2 * CHUNKS,)),
        dma((2,)), dma((2,)), dma(()), dma(()),
        dma(()), dma(()), dma((G,)), dma((G,)),
        dma((NP,)), dma((NP,)),
        dma((ring,)), dma((ring,)), dma((ring,)), dma((ring,)),
        dma((NP,)), dma((NP,)), dma((NS.bit_length(),)), dma((NS.bit_length(),)),
        dma((CHUNKS * NP,)), dma((CHUNKS * NP,)), dma((CHUNKS * NP,)), dma((CHUNKS * NP,)),
    ]
    anywhere = pl.BlockSpec(memory_space=pltpu.HBM)
    vmem = pl.BlockSpec(memory_space=pltpu.VMEM)
    return pl.pallas_call(
        functools.partial(stein_kernel, (NP, NS, RB, TOK, D, FF, POOL)),
        out_shape=jax.ShapeDtypeStruct((CHUNKS, NP, RB, LANES), BF16),
        in_specs=[anywhere] * 5,
        out_specs=vmem,
        scratch_shapes=scratch,
        compiler_params=pltpu.CompilerParams(
            collective_id=0, has_side_effects=True, vmem_limit_bytes=56 * 1024 * 1024
        ),
        name="stein",
    )(kernel_scale, batch_index.reshape(1, TOK), flat_w, pool, cotangent)


def adam_kernel(NT, parts, moved_ref, w_ref, m_ref, v_ref, new_w, new_m, new_v, transport_ref, out, sems):
    NP, rows = moved_ref.shape[1:3]
    TC = NT // 2 // CHUNKS
    part_rows = rows // parts
    size = part_rows * 2 * NT
    copies = []
    for part in range(parts):
        span = pl.ds(part * size, size)
        for k in range(CHUNKS):
            for q in range(NP):
                o, half = q // 2, q % 2
                t = (half * CHUNKS + k) * TC + o // 2
                piece = moved_ref[k, q, part * part_rows:(part + 1) * part_rows, :].astype(F32)
                out[0, pl.ds(part * size + 2 * t + o % 2, part_rows, stride=2 * NT), :] = piece
        transport = out[0, span, :]
        new_first = 0.9 * m_ref[span, :] - 0.1 * transport
        new_second = 0.999 * v_ref[span, :] + 0.001 * transport * transport
        out[1, span, :] = new_first
        out[2, span, :] = new_second
        out[3, span, :] = w_ref[span, :] - 0.01 * new_first / (jnp.sqrt(new_second) + 1e-08)
        for n, target in enumerate((transport_ref, new_m, new_v, new_w)):
            copy = pltpu.make_async_copy(out.at[n, span], target.at[span], sems.at[n, part])
            copy.start()
            copies.append(copy)
    for copy in copies:
        copy.wait()


def adam(moved, flat_w, flat_m, flat_v):
    RB, lanes = moved.shape[2:]
    parts = max(RB // 16, 1)
    shape = jax.ShapeDtypeStruct(flat_w.shape, F32)
    return pl.pallas_call(
        functools.partial(adam_kernel, flat_w.shape[0] // RB // 2, parts),
        out_shape=(shape,) * 4,
        in_specs=[pl.BlockSpec(memory_space=pltpu.VMEM)] * 4,
        out_specs=(pl.BlockSpec(memory_space=pltpu.HBM),) * 4,
        scratch_shapes=[pltpu.VMEM((4,) + flat_w.shape, F32), pltpu.SemaphoreType.DMA((4, parts))],
        compiler_params=pltpu.CompilerParams(vmem_limit_bytes=16 * 1024 * 1024),
        name="adam",
    )(moved, flat_w, flat_m, flat_v)


def local(NP, NS, pool, batch_index, kernel_scale, cotangent, weights, first_moment, second_moment):
    rows, pair, hidden_units = weights.shape[1:]

    def flatten(a):
        return a.reshape(rows, pair, hidden_units // LANES, LANES).transpose(0, 2, 1, 3).reshape(-1, LANES)

    def unflatten(a):
        a = a.reshape(rows, hidden_units // LANES, pair, LANES).transpose(0, 2, 1, 3)
        return a.reshape(1, rows, pair, hidden_units)

    flat_w = flatten(weights[0])
    moved = stein_transport(NP, NS, kernel_scale, batch_index, flat_w, pool, cotangent[0])
    outs = adam(moved, flat_w, flatten(first_moment[0]), flatten(second_moment[0]))
    return tuple(unflatten(a) for a in outs)


def solution(mesh):
    placed = (
        P("shard", None),
        P("shard"),
        P(),
        P("particle", "shard", None),
        P("particle", "shard", None, None),
        P("particle", "shard", None, None),
        P("particle", "shard", None, None),
    )
    return jax.shard_map(
        functools.partial(local, mesh.shape["particle"], mesh.shape["shard"]),
        mesh=mesh,
        in_specs=placed,
        out_specs=(P("particle", "shard", None, None),) * 4,
        check_vma=False,
    )
```
